256 devices in a mesh: blk: 128 (over y_hi, x, z, core), sub: 2 (over y_lo).
Axes of the slice: x: 4, y: 4 (y_hi: 2, y_lo: 2; y = y_hi * 2 + y_lo), z: 8, core: 2. Of those that a mesh axis runs over, the one named last changes fastest.
Arguments:
- adjoint_start: float32 [5, 4096, 16, 128], P(None, 'blk', 'sub'), may hold values from -6 to 6
- objective_grad: float32 [5, 4096, 16, 128], P(None, 'blk', 'sub'), may hold values from -6 to 6
- flux_jacobian: bfloat16 [3, 5, 5, 4096, 16, 128], P(None, None, None, 'blk', 'sub'), may hold values from -3 to 3
- stab_block: bfloat16 [5, 5, 4096, 16, 128], P(None, None, 'blk', 'sub'), as said below
- precond_block: bfloat16 [5, 5, 4096, 16, 128], P(None, None, 'blk', 'sub'), as said below
- wall_weight: float32 [5, 2], replicated, may hold values from -4 to 4
- wall_geometry: bfloat16 [524288, 2, 128], P('blk'), may hold values from -6 to 6
- face_patch: int32 [524288], P('blk'), may hold values from 0 to 2047
- patch_slot: int32 [2048], replicated, may hold values from 0 to 2047, each once
Outputs:
- adjoint_state: float32 [5, 4096, 16, 128], P(None, 'blk', 'sub')
- patch_sens: float32 [2048, 128], P('blk')
The draws below stay inside these ranges and needn't reach their ends.
Inputs may be any that keep to these rules, and one draw needn't show every extreme that they name: `stab_block`: diagonal entries between 2 and 4, off-diagonal ones smaller in magnitude than 2. `precond_block`: diagonal entries between 0.15 and 0.3, off-diagonal ones smaller in magnitude than 0.15.
All inputs are finite; a program needn't handle non-finite values.
Results may differ from the reference program's by a relative error of at most 0.0003.
Values sent between devices are 32-bit elements; how exact they have to be, the bound alone decides.
A program may use at most 128 MiB of HBM per device.

```python
import math
import jax
import jax.numpy as jnp
import numpy as np

NVAR = 5
CA = 32
CC = 128
KS = 128
NA = 4096
NN = 16
FACES = 524288
PATCHES = 2048


def banded_block(key, lower, upper, spread):
    first, second = jax.random.split(key)
    dims = (NVAR, NVAR, NA, NN, CC)
    diagonal = jax.random.uniform(first, dims, jnp.float32, lower, upper)
    rough = jnp.clip(jax.random.normal(second, dims, jnp.float32), -2.5, 2.5) * spread
    identity = jnp.eye(NVAR, dtype=jnp.float32)[:, :, None, None, None]
    return (identity * diagonal + (1.0 - identity) * rough).astype(jnp.bfloat16)


def draw_stab_block(key, part):
    return banded_block(jax.random.fold_in(key, 11), 2.0, 4.0, 0.4)


def draw_precond_block(key, part):
    return banded_block(jax.random.fold_in(key, 23), 0.15, 0.3, 0.05)


def with_ends(values, rng, least, high):
    extent = values.shape
    place = [jax.random.randint(jax.random.fold_in(rng, axis), (), 0, extent[axis]) for axis in range(len(extent))]
    values = values.at[tuple(place)].set(least)
    longest = extent.index(max(extent))
    place[longest] = (place[longest] + 1) % extent[longest]
    return values.at[tuple(place)].set(high)


def steps_of(key, shape, pieces, low, high):
    factor_of, own = 1.0, jax.random.fold_in(key, 6)
    for axis_at, parts in pieces:
        heights = jnp.exp(jax.random.uniform(jax.random.fold_in(own, axis_at), (parts,), jnp.float32, low / len(pieces), high / len(pieces)))
        factor_of = factor_of * jnp.repeat(heights, shape[axis_at] // parts).reshape([-1 if axis == axis_at else 1 for axis in range(len(shape))])
    return factor_of


def cumulative_ranks(number_of, lean):
    weights = [(1 << 20) // math.isqrt(rank ** lean) + 1 for rank in range(1, number_of + 1)]
    width = 1 + sum(weights) // (1 << 30)
    return np.cumsum(np.array([max(1, weight // width) for weight in weights]))


def ranked(rng, extent, number_of, slope):
    listing = cumulative_ranks(number_of, slope)
    lot = jax.random.randint(jax.random.fold_in(rng, 1), extent, 0, int(listing[number_of - 1]))
    standing = jnp.searchsorted(jnp.asarray(listing, jnp.int32), lot, side="right")
    return jax.random.permutation(jax.random.fold_in(rng, 2), number_of)[standing].astype(jnp.int32)


def noise(stream_key, shape, deviation, reach, pieces=(), kind=jnp.bfloat16):
    result = deviation * jax.random.normal(stream_key, shape, jnp.float32)
    if pieces:
        result = result * steps_of(stream_key, shape, pieces, -0.22, 0.18)
    return jnp.clip(result, -reach, reach).astype(kind)


def setup_inputs(seed: int = 0) -> dict:
    seeds = jax.random.split(jax.random.key(seed), 10)
    adjoint_start = noise(seeds[0], (NVAR, NA, NN, CC), 1.0, 6.0, ((1, 128), (2, 2)), jnp.float32)
    objective_grad = noise(seeds[1], (NVAR, NA, NN, CC), 1.0, 6.0, ((1, 128), (2, 2)), jnp.float32)
    flux_jacobian = noise(seeds[2], (3, NVAR, NVAR, NA, NN, CC), 0.5, 3.0, ((3, 128), (4, 2)))
    stab_block = draw_stab_block(jax.random.fold_in(seeds[9], 71), 0)
    precond_block = draw_precond_block(jax.random.fold_in(seeds[9], 71), 0)
    wall_weight = noise(seeds[5], (NVAR, 2), 1.0, 4.0, (), jnp.float32)
    wall_geometry = noise(seeds[6], (FACES, 2, KS), 1.0, 6.0, ((0, 128),))
    face_patch = with_ends(ranked(seeds[7], (FACES,), PATCHES, 1), jax.random.fold_in(seeds[7], 3), 0, PATCHES - 1).astype(jnp.int32)
    patch_slot = jax.random.permutation(seeds[8], PATCHES).astype(jnp.int32)
    return {"adjoint_start": adjoint_start, "objective_grad": objective_grad, "flux_jacobian": flux_jacobian, "stab_block": stab_block, "precond_block": precond_block, "wall_weight": wall_weight, "wall_geometry": wall_geometry, "face_patch": face_patch, "patch_slot": patch_slot}


def transposed(matrix, field):
    return jnp.sum(matrix * field[:, None], axis=0)


def sweep(state, flux_jacobian, stab_block, precond_block, objective_grad):
    padded = jnp.pad(state, ((0, 0), (1, 1), (1, 1), (1, 1)))
    diff_a = padded[:, :-2, 1:-1, 1:-1] - padded[:, 2:, 1:-1, 1:-1]
    diff_n = padded[:, 1:-1, :-2, 1:-1] - padded[:, 1:-1, 2:, 1:-1]
    diff_c = padded[:, 1:-1, 1:-1, :-2] - padded[:, 1:-1, 1:-1, 2:]
    jac = flux_jacobian.astype(jnp.float32)
    resid = objective_grad - transposed(stab_block.astype(jnp.float32), state)
    resid = resid - 0.5 * (transposed(jac[0], diff_a) + transposed(jac[1], diff_n) + transposed(jac[2], diff_c))
    return state + jnp.sum(precond_block.astype(jnp.float32) * resid[None, :], axis=1)


def reference(adjoint_start, objective_grad, flux_jacobian, stab_block, precond_block, wall_weight, wall_geometry, face_patch, patch_slot):
    state = adjoint_start
    for index in range(2):
        state = sweep(state, flux_jacobian, stab_block, precond_block, objective_grad)
    parity = (jnp.arange(NA, dtype=jnp.int32) // CA) % 2
    wall_cells = jnp.where(parity[None, :, None] == 1, state[:, :, NN - 1, :], state[:, :, 0, :])
    wall_psi = wall_cells.reshape(NVAR, -1)
    sens_p = jnp.sum(wall_weight[:, 0:1] * wall_psi, axis=0)
    sens_t = jnp.sum(wall_weight[:, 1:2] * wall_psi, axis=0)
    geometry = wall_geometry.astype(jnp.float32)
    contribution = sens_p[:, None] * geometry[:, 0, :] + sens_t[:, None] * geometry[:, 1, :]
    slots = patch_slot[face_patch].astype(jnp.int32)
    patch_sens = jax.ops.segment_sum(contribution, slots, num_segments=PATCHES)
    return state, patch_sens
```

```python
import functools

import jax
import jax.numpy as jnp
from jax import lax
from jax.experimental import pallas as pl
from jax.experimental.pallas import tpu as pltpu
from jax.sharding import PartitionSpec as P

MESH = pl.DeviceIdType.MESH
F32 = jnp.float32
BF16 = jnp.bfloat16

NV = 5
NX, NZ = 4, 8


def kernel(
    start_h, grad_h, jac_h, stab_h, prec_h, weight_s, geom_h, face_v, slot_v,
    state_h, patch_v,
    psi0, psi1, psi2, grad, jac, stab, prec, geom, geom32, onehot, key, contrib, acc,
    nsend0, nrecv0, nsend1, nrecv1, sens_loc, sens,
    core_in, x_out, x_in, z_out, z_in, y_out, y_in,
    load_sem, out_sem, a_send, a_recv, n_send, n_recv, s_send, s_recv,
    c_send, c_recv, x_send, x_recv, z_send, z_recv, y_send, y_recv,
):
    blk, sub = lax.axis_index("blk"), lax.axis_index("sub")
    n_blk = lax.axis_size("blk")
    core = lax.rem(blk, 2)
    z = lax.rem(blk // 2, NZ)
    x = lax.rem(blk // (2 * NZ), NX)
    yh = blk // (2 * NZ * NX)

    def at(yh_, x_, z_, core_):
        return ((yh_ * NX + x_) * NZ + z_) * 2 + core_

    core_peer = (at(yh, x, z, 1 - core), sub)
    x_peer = [(at(yh, lax.rem(x + d, NX), z, core), sub) for d in range(NX)]
    z_peer = [(at(yh, x, lax.rem(z + d, NZ), core), sub) for d in range(NZ)]
    y_peer = [(at(1 - yh, x, z, core), sub), (at(1 - yh, x, z, core), 1 - sub), (blk, 1 - sub)]
    partner = (blk, 1 - sub)
    has_left, has_right = blk > 0, blk < n_blk - 1
    other = jnp.where(core == 1, blk + 1, blk - 1)
    has_other = jnp.logical_and(other >= 0, other < n_blk)

    loads = [
        pltpu.make_async_copy(start_h, psi0.at[:, 8:264, :], load_sem.at[0]),
        pltpu.make_async_copy(geom_h, geom, load_sem.at[1]),
        pltpu.make_async_copy(grad_h, grad, load_sem.at[2]),
        pltpu.make_async_copy(jac_h.at[0:25], jac.at[0:25], load_sem.at[3]),
        pltpu.make_async_copy(jac_h.at[25:50], jac.at[25:50], load_sem.at[4]),
        pltpu.make_async_copy(jac_h.at[50:75], jac.at[50:75], load_sem.at[5]),
        pltpu.make_async_copy(stab_h, stab, load_sem.at[6]),
        pltpu.make_async_copy(prec_h, prec, load_sem.at[7]),
    ]
    for load in loads:
        load.start()

    barrier = pltpu.get_barrier_semaphore()
    peers = [core_peer] + x_peer[1:] + z_peer[1:] + y_peer
    for peer in peers:
        pl.semaphore_signal(barrier, inc=1, device_id=peer, device_id_type=MESH)

    @pl.when(has_other)
    def _():
        pl.semaphore_signal(barrier, inc=1, device_id=(other, sub), device_id_type=MESH)

    zero_plane = jnp.zeros((NV, 8, 128), F32)
    for buf in (psi0, psi1):
        @pl.when(jnp.logical_not(has_left))
        def _():
            buf[:, 0:8, :] = zero_plane

        @pl.when(jnp.logical_not(has_right))
        def _():
            buf[:, 264:272, :] = zero_plane

    loads[0].wait()

    def edge_row(plane):
        return jnp.where(sub == 0, plane[7:8], plane[0:1])

    def pick0(a, carry):
        for v in range(NV):
            nsend0[v, a] = edge_row(psi0[v, pl.ds(pl.multiple_of(8 * a + 8, 8), 8), :])
        return carry

    lax.fori_loop(0, 32, pick0, 0)

    pl.semaphore_wait(barrier, len(peers) + has_other.astype(jnp.int32))

    def a_copies(buf, base):
        right = pltpu.make_async_remote_copy(
            src_ref=buf.at[:, 256:264, :], dst_ref=buf.at[:, 0:8, :],
            send_sem=a_send.at[base], recv_sem=a_recv.at[base],
            device_id=(jnp.minimum(blk + 1, n_blk - 1), sub), device_id_type=MESH)
        left = pltpu.make_async_remote_copy(
            src_ref=buf.at[:, 8:16, :], dst_ref=buf.at[:, 264:272, :],
            send_sem=a_send.at[base + 1], recv_sem=a_recv.at[base + 1],
            device_id=(jnp.maximum(blk - 1, 0), sub), device_id_type=MESH)
        return right, left

    def start_a(buf, base):
        right, left = a_copies(buf, base)

        @pl.when(has_right)
        def _():
            right.start()

        @pl.when(has_left)
        def _():
            left.start()

    def wait_a_recv(buf, base):
        right, left = a_copies(buf, base)

        @pl.when(has_left)
        def _():
            right.wait_recv()

        @pl.when(has_right)
        def _():
            left.wait_recv()

    def wait_a_send(buf, base):
        right, left = a_copies(buf, base)

        @pl.when(has_right)
        def _():
            right.wait_send()

        @pl.when(has_left)
        def _():
            left.wait_send()

    n_copy0 = pltpu.make_async_remote_copy(
        src_ref=nsend0, dst_ref=nrecv0, send_sem=n_send.at[4], recv_sem=n_recv.at[4],
        device_id=partner, device_id_type=MESH)
    n_copy0.start()
    start_a(psi0, 0)

    table = slot_v[...]
    for g in range(4):
        patch = face_v[8 * g:8 * g + 8, :]
        lane, high = patch & 127, patch >> 7
        found = jnp.zeros((8, 128), jnp.int32)
        for j in range(16):
            line = jnp.broadcast_to(table[j:j + 1, :], (8, 128))
            found = jnp.where(high == j, jnp.take_along_axis(line, lane, axis=1), found)
        j_, sub_, core_ = found & 7, (found >> 3) & 1, (found >> 4) & 1
        z_, x_, yh_ = (found >> 5) & 7, (found >> 8) & 3, (found >> 10) & 1
        row = (core_ << 9) + (x_ << 7) + (z_ << 4) + (yh_ << 3) + j_
        key[8 * g:8 * g + 8, :] = jnp.where(sub_ == sub, row, -1)

    def fill(i, carry):
        a = lax.rem(i + 6, 32)
        k = jnp.broadcast_to(key[pl.ds(a, 1), :], (16, 128))
        base = lax.broadcasted_iota(jnp.int32, (16, 128), 0)
        for m in range(64):
            hit = (base + 16 * m) == k
            onehot[16 * m:16 * m + 16, pl.ds(pl.multiple_of(i * 128, 128), 128)] = jnp.where(hit, 1.0, 0.0).astype(BF16)
        return carry

    lax.fori_loop(0, 32, fill, 0)

    loads[1].wait()

    def widen(a, carry):
        geom32[a] = geom[pl.ds(pl.multiple_of(a * 256, 256), 256), :].astype(F32)
        return carry

    lax.fori_loop(0, 32, widen, 0)

    sub_iota = lax.broadcasted_iota(jnp.int32, (16, 128), 0) & 7
    lane_iota = lax.broadcasted_iota(jnp.int32, (16, 128), 1)
    edge_n = jnp.where(
        sub == 0, jnp.where(sub_iota == 7, -1.0, 0.0), jnp.where(sub_iota == 0, 1.0, 0.0)).astype(F32)

    def sweep_pair(p, buf, halo, halo_row):
        rows = pl.ds(pl.multiple_of(16 * p, 16), 16)
        stab_acc, jac_acc, psi = [None] * NV, [None] * NV, [None] * NV

        def add(total, term):
            return term if total is None else total + term

        for u in range(NV):
            four = buf[u, pl.ds(pl.multiple_of(16 * p, 16), 32), :]
            here = four[8:24]
            psi[u] = here
            d_a = four[0:16] - four[16:32]
            before = jnp.concatenate([pltpu.roll(here[0:8], 1, 0), pltpu.roll(here[8:16], 1, 0)], 0)
            after = jnp.concatenate([pltpu.roll(here[0:8], 7, 0), pltpu.roll(here[8:16], 7, 0)], 0)
            ghost = jnp.concatenate([jnp.broadcast_to(halo[u, halo_row], (8, 128)),
                                     jnp.broadcast_to(halo[u, halo_row + 1], (8, 128))], 0)
            d_n = jnp.where(sub_iota == 0, 0.0, before) - jnp.where(sub_iota == 7, 0.0, after) + edge_n * ghost
            d_c = (jnp.where(lane_iota == 0, 0.0, pltpu.roll(here, 1, 1))
                   - jnp.where(lane_iota == 127, 0.0, pltpu.roll(here, 127, 1)))
            for v in range(NV):
                i = u * NV + v
                stab_acc[v] = add(stab_acc[v], stab[i, rows, :].astype(F32) * here)
                jac_acc[v] = add(jac_acc[v], jac[i, rows, :].astype(F32) * d_a)
                jac_acc[v] = jac_acc[v] + jac[25 + i, rows, :].astype(F32) * d_n
                jac_acc[v] = jac_acc[v] + jac[50 + i, rows, :].astype(F32) * d_c
        resid = [grad[v, rows, :] - stab_acc[v] - 0.5 * jac_acc[v] for v in range(NV)]
        result = []
        for u in range(NV):
            step = None
            for v in range(NV):
                step = add(step, prec[u * NV + v, rows, :].astype(F32) * resid[v])
            result.append(psi[u] + step)
        return result

    for load in loads[2:]:
        load.wait()
    n_copy0.wait_recv()
    wait_a_recv(psi0, 0)

    def n_copy1(k):
        part = pl.ds(pl.multiple_of(8 * k, 8), 8)
        return pltpu.make_async_remote_copy(
            src_ref=nsend1.at[:, part], dst_ref=nrecv1.at[:, part], send_sem=n_send.at[k], recv_sem=n_recv.at[k],
            device_id=partner, device_id_type=MESH)

    def first_part(k, carry):
        def pair(i, carry):
            p = lax.rem(i + 15, 16)
            new = sweep_pair(p, psi0, nrecv0, 2 * p)
            for v in range(NV):
                psi1[v, pl.ds(pl.multiple_of(16 * p + 8, 8), 16), :] = new[v]
                nsend1[v, 2 * i] = edge_row(new[v][0:8])
                nsend1[v, 2 * i + 1] = edge_row(new[v][8:16])
            return carry

        lax.fori_loop(4 * k, 4 * k + 4, pair, 0)
        n_copy1(k).start()

        @pl.when(k == 0)
        def _():
            start_a(psi1, 2)

        return carry

    lax.fori_loop(0, 4, first_part, 0)

    is_wall = core == sub
    not_wall = jnp.logical_not(is_wall)

    def s_copy(k):
        part = pl.ds(pl.multiple_of(8 * k, 8), 8)
        return pltpu.make_async_remote_copy(
            src_ref=sens_loc.at[:, part, :], dst_ref=sens.at[:, part, :], send_sem=s_send.at[k], recv_sem=s_recv.at[k],
            device_id=partner, device_id_type=MESH)

    def wall_row(plane):
        return jnp.where(sub == 0, plane[0:1], plane[7:8])

    def second_part(k, carry):
        n_copy1(lax.rem(k + 1, 4)).wait_recv()

        @pl.when(k == 3)
        def _():
            wait_a_recv(psi1, 2)

        def pair(i, carry):
            p = lax.rem(i + 3, 16)
            new = sweep_pair(p, psi1, nrecv1, 2 * lax.rem(i + 4, 16))
            for v in range(NV):
                psi2[v, pl.ds(pl.multiple_of(16 * p, 16), 16), :] = new[v]
            for j in range(2):
                total = weight_s[0, j] * new[0]
                for v in range(1, NV):
                    total = total + weight_s[v, j] * new[v]
                sens_loc[j, pl.ds(2 * i, 1), :] = wall_row(total[0:8])
                sens_loc[j, pl.ds(2 * i + 1, 1), :] = wall_row(total[8:16])
            return carry

        lax.fori_loop(4 * k, 4 * k + 4, pair, 0)

        @pl.when(is_wall)
        def _():
            s_copy(k).start()
            part = pl.ds(pl.multiple_of(8 * k, 8), 8)
            sens[:, part, :] = sens_loc[:, part, :]

        return carry

    lax.fori_loop(0, 4, second_part, 0)
    state_copy = pltpu.make_async_copy(psi2, state_h, out_sem)
    state_copy.start()

    def make_contrib(k):
        @pl.when(not_wall)
        def _():
            s_copy(k).wait_recv()

        part = pl.ds(pl.multiple_of(8 * k, 8), 8)
        pressure = jnp.transpose(sens[0, part, :])
        shear = jnp.transpose(sens[1, part, :])
        for r in range(8):
            a = lax.rem(8 * k + 6 + r, 32)
            g0 = geom32[a, pl.ds(0, 128, 2), :]
            g1 = geom32[a, pl.ds(1, 128, 2), :]
            c = pressure[:, r:r + 1] * g0 + shear[:, r:r + 1] * g1
            hi = c.astype(BF16)
            lo = (c - hi.astype(F32)).astype(BF16)
            contrib[128 * r:128 * r + 128, 0:128] = hi
            contrib[128 * r:128 * r + 128, 128:256] = lo

    def product(row, k):
        part = onehot[pl.ds(pl.multiple_of(row, 128), 128), pl.ds(pl.multiple_of(k * 1024, 1024), 1024)]
        both = jnp.dot(part, contrib[...], preferred_element_type=F32)
        return both[:, 0:128] + both[:, 128:256]

    acc[...] = jnp.zeros((1024, 128), F32)

    def quarter(k, carry):
        make_contrib(k)

        def block(m, carry):
            rows = pl.ds(pl.multiple_of(m * 128, 128), 128)
            acc[rows, :] += product(m * 128, k)
            return carry

        lax.fori_loop(0, 8, block, 0)
        return carry

    lax.fori_loop(0, 3, quarter, 0)
    make_contrib(3)

    def order(k):
        return lax.rem(k + 2, 4)

    def c_copy(k):
        start = (1 - core) * 512 + lax.rem(x + order(k), NX) * 128
        return pltpu.make_async_remote_copy(
            src_ref=acc.at[pl.ds(pl.multiple_of(start, 128), 128), :], dst_ref=core_in.at[k],
            send_sem=c_send.at[k], recv_sem=c_recv.at[k], device_id=core_peer, device_id_type=MESH)

    def x_copy(k):
        peer = (at(yh, lax.rem(x + order(k), NX), z, core), sub)
        return pltpu.make_async_remote_copy(
            src_ref=x_out.at[k], dst_ref=x_in.at[k],
            send_sem=x_send.at[k], recv_sem=x_recv.at[k], device_id=peer, device_id_type=MESH)

    def away(k, carry):
        start = (1 - core) * 512 + lax.rem(x + order(k), NX) * 128
        rows = pl.ds(pl.multiple_of(start, 128), 128)
        acc[rows, :] += product(start, 3)
        c_copy(k).start()
        return carry

    lax.fori_loop(0, 4, away, 0)

    def kept(k, carry):
        start = core * 512 + lax.rem(x + order(k), NX) * 128
        rows = pl.ds(pl.multiple_of(start, 128), 128)
        mine = acc[rows, :] + product(start, 3)
        c_copy(k).wait_recv()
        x_out[k] = mine + core_in[k]

        @pl.when(order(k) != 0)
        def _():
            x_copy(k).start()

        return carry

    lax.fori_loop(0, 4, kept, 0)
    for k in (1, 3, 0):
        x_copy(k).wait_recv()
    z_out[...] = x_out[2] + x_in[0] + x_in[1] + x_in[3]

    def z_copy(d):
        dest = lax.rem(z + d, NZ)
        peer = (at(yh, x, dest, core), sub)
        return pltpu.make_async_remote_copy(
            src_ref=z_out.at[pl.ds(pl.multiple_of(dest * 16, 16), 16), :], dst_ref=z_in.at[d - 1],
            send_sem=z_send.at[d - 1], recv_sem=z_recv.at[d - 1], device_id=peer, device_id_type=MESH)

    for d in (4, 3, 5, 2, 6, 1, 7):
        z_copy(d).start()
    for d in range(1, NZ):
        z_copy(d).wait_recv()
    total = z_out[pl.ds(pl.multiple_of(z * 16, 16), 16), :]
    for d in range(NZ - 1):
        total = total + z_in[d]
    y_out[...] = total

    y_rows = [1 - yh, 1 - yh, yh]

    def y_copy(k):
        return pltpu.make_async_remote_copy(
            src_ref=y_out.at[pl.ds(pl.multiple_of(y_rows[k] * 8, 8), 8), :], dst_ref=y_in.at[k],
            send_sem=y_send.at[k], recv_sem=y_recv.at[k], device_id=y_peer[k], device_id_type=MESH)

    for k in range(3):
        y_copy(k).start()
    for k in range(3):
        y_copy(k).wait_recv()
    mine = pl.ds(pl.multiple_of(8 * sub, 8), 8)
    others = pl.ds(pl.multiple_of(8 * (1 - sub), 8), 8)
    patch_v[mine, :] = y_out[pl.ds(pl.multiple_of(yh * 8, 8), 8), :] + y_in[0]
    patch_v[others, :] = y_in[1] + y_in[2]

    n_copy0.wait_send()
    wait_a_send(psi0, 0)
    wait_a_send(psi1, 2)
    for k in range(4):
        n_copy1(k).wait_send()

    @pl.when(is_wall)
    def _():
        for k in range(4):
            s_copy(k).wait_send()

    for k in range(4):
        c_copy(k).wait_send()
    for k in (0, 1, 3):
        x_copy(k).wait_send()
    for d in range(1, NZ):
        z_copy(d).wait_send()
    for k in range(3):
        y_copy(k).wait_send()
    state_copy.wait()


def local(
    adjoint_start, objective_grad, flux_jacobian, stab_block, precond_block,
    wall_weight, wall_geometry, face_patch, patch_slot,
):
    any_, vmem, smem = (pl.BlockSpec(memory_space=m) for m in (pl.ANY, pltpu.VMEM, pltpu.SMEM))
    dma = pltpu.SemaphoreType.DMA
    state, patch = pl.pallas_call(
        kernel,
        out_shape=(jax.ShapeDtypeStruct((NV, 256, 128), F32), jax.ShapeDtypeStruct((16, 128), F32)),
        in_specs=[any_, any_, any_, any_, any_, smem, any_, vmem, vmem],
        out_specs=(any_, vmem),
        scratch_shapes=[
            pltpu.VMEM((NV, 272, 128), F32),
            pltpu.VMEM((NV, 272, 128), F32),
            pltpu.VMEM((NV, 256, 128), F32),
            pltpu.VMEM((NV, 256, 128), F32),
            pltpu.VMEM((75, 256, 128), BF16),
            pltpu.VMEM((25, 256, 128), BF16),
            pltpu.VMEM((25, 256, 128), BF16),
            pltpu.VMEM((8192, 128), BF16),
            pltpu.VMEM((32, 256, 128), F32),
            pltpu.VMEM((1024, 4096), BF16),
            pltpu.VMEM((32, 128), jnp.int32),
            pltpu.VMEM((1024, 256), BF16),
            pltpu.VMEM((1024, 128), F32),
            pltpu.VMEM((NV, 32, 1, 128), F32),
            pltpu.VMEM((NV, 32, 1, 128), F32),
            pltpu.VMEM((NV, 32, 1, 128), F32),
            pltpu.VMEM((NV, 32, 1, 128), F32),
            pltpu.VMEM((2, 32, 128), F32),
            pltpu.VMEM((2, 32, 128), F32),
            pltpu.VMEM((4, 128, 128), F32),
            pltpu.VMEM((4, 128, 128), F32),
            pltpu.VMEM((4, 128, 128), F32),
            pltpu.VMEM((128, 128), F32),
            pltpu.VMEM((NZ - 1, 16, 128), F32),
            pltpu.VMEM((16, 128), F32),
            pltpu.VMEM((3, 8, 128), F32),
            dma((8,)), dma,
            dma((4,)), dma((4,)),
            dma((5,)), dma((5,)),
            dma((4,)), dma((4,)),
            dma((4,)), dma((4,)),
            dma((4,)), dma((4,)),
            dma((NZ - 1,)), dma((NZ - 1,)),
            dma((3,)), dma((3,)),
        ],
        compiler_params=pltpu.CompilerParams(
            collective_id=0, has_side_effects=True, vmem_limit_bytes=60 * 1024 * 1024),
    )(
        adjoint_start.reshape(NV, 256, 128),
        objective_grad.reshape(NV, 256, 128),
        flux_jacobian.reshape(75, 256, 128),
        stab_block.reshape(25, 256, 128),
        precond_block.reshape(25, 256, 128),
        wall_weight,
        wall_geometry.reshape(8192, 128),
        face_patch.reshape(32, 128),
        patch_slot.reshape(16, 128),
    )
    return state.reshape(NV, 32, 8, 128), patch


def solution(mesh):
    return jax.shard_map(
        local,
        mesh=mesh,
        in_specs=(
            P(None, "blk", "sub", None),
            P(None, "blk", "sub", None),
            P(None, None, None, "blk", "sub", None),
            P(None, None, "blk", "sub", None),
            P(None, None, "blk", "sub", None),
            P(),
            P("blk", None, None),
            P("blk"),
            P(),
        ),
        out_specs=(P(None, "blk", "sub", None), P("blk", None)),
        check_vma=False,
    )
```

```python
import functools

import jax
import jax.numpy as jnp
from jax import lax
from jax.experimental import pallas as pl
from jax.experimental.pallas import tpu as pltpu
from jax.sharding import PartitionSpec as P

MESH = pl.DeviceIdType.MESH
F32 = jnp.float32
BF16 = jnp.bfloat16

NV = 5
PARTS = ((16, 80), (0, 16), (240, 256), (80, 176), (176, 240))
PART_OF = ((0,), (1, 2), (3,), (4,))
GHOSTS = ((4, 12), (0, 4), (12, 24), (24, 32))
NX, NZ = 4, 8


def kernel(
    start_h, grad_h, jac_h, stab_h, prec_h, weight_h, geom_h, face_h, slot_h,
    state_h, patch_v,
    psi0, psi1, psi2, grad, jac, stab, prec, geom, weight_s, face_v, slot_v, geom32, onehot, key, contrib, acc,
    nsend0, nrecv0, nsend1, nrecv1, sens_loc, sens,
    core_in, x_out, x_in, z_out, z_in, y_out, y_in,
    load_sem, part_sem, out_sem, a_send, a_recv, n0_send, n0_recv, n_send, n_recv, s_send, s_recv,
    c_send, c_recv, x_send, x_recv, z_send, z_recv, y_send, y_recv,
):
    blk, sub = lax.axis_index("blk"), lax.axis_index("sub")
    n_blk = lax.axis_size("blk")
    core = lax.rem(blk, 2)
    z = lax.rem(blk // 2, NZ)
    x = lax.rem(blk // (2 * NZ), NX)
    yh = blk // (2 * NZ * NX)

    def at(yh_, x_, z_, core_):
        return ((yh_ * NX + x_) * NZ + z_) * 2 + core_

    core_peer = (at(yh, x, z, 1 - core), sub)
    x_peer = [(at(yh, lax.rem(x + d, NX), z, core), sub) for d in range(NX)]
    z_peer = [(at(yh, x, lax.rem(z + d, NZ), core), sub) for d in range(NZ)]
    y_peer = [(at(1 - yh, x, z, core), sub), (at(1 - yh, x, z, core), 1 - sub), (blk, 1 - sub)]
    partner = (blk, 1 - sub)
    has_left, has_right = blk > 0, blk < n_blk - 1
    other = jnp.where(core == 1, blk + 1, blk - 1)
    has_other = jnp.logical_and(other >= 0, other < n_blk)

    barrier = pltpu.get_barrier_semaphore()
    peers = [core_peer] + x_peer[1:] + z_peer[1:] + y_peer
    for peer in peers:
        pl.semaphore_signal(barrier, inc=1, device_id=peer, device_id_type=MESH)

    @pl.when(has_other)
    def _():
        pl.semaphore_signal(barrier, inc=1, device_id=(other, sub), device_id_type=MESH)

    loads = [
        pltpu.make_async_copy(start_h, psi0.at[:, 8:264, :], load_sem.at[0]),
        pltpu.make_async_copy(face_h, face_v, load_sem.at[1]),
        pltpu.make_async_copy(slot_h, slot_v, load_sem.at[2]),
        pltpu.make_async_copy(weight_h, weight_s, load_sem.at[3]),
        pltpu.make_async_copy(geom_h, geom, load_sem.at[4]),
    ]
    parts = []
    for n, (low, high) in enumerate(PARTS):
        rows = slice(low, high)
        parts.append([
            pltpu.make_async_copy(far.at[:, rows, :], near.at[:, rows, :], part_sem.at[4 * n + j])
            for j, (far, near) in enumerate(((jac_h, jac), (stab_h, stab), (prec_h, prec), (grad_h, grad)))
        ])
    for load in loads[:4]:
        load.start()
    for part in parts:
        for load in part:
            load.start(priority=1)
    loads[4].start(priority=1)

    zero_plane = jnp.zeros((NV, 8, 128), F32)
    for buf in (psi0, psi1):
        @pl.when(jnp.logical_not(has_left))
        def _():
            buf[:, 0:8, :] = zero_plane

        @pl.when(jnp.logical_not(has_right))
        def _():
            buf[:, 264:272, :] = zero_plane

    loads[0].wait()

    def edge_row(plane):
        return jnp.where(sub == 0, plane[7:8], plane[0:1])

    def pick0(q, carry):
        a = lax.rem(q + 30, 32)
        for v in range(NV):
            nsend0[v, q] = edge_row(psi0[v, pl.ds(pl.multiple_of(8 * a + 8, 8), 8), :])
        return carry

    lax.fori_loop(0, 32, pick0, 0)

    pl.semaphore_wait(barrier, len(peers) + has_other.astype(jnp.int32))

    def a_copies(buf, base):
        right = pltpu.make_async_remote_copy(
            src_ref=buf.at[:, 256:264, :], dst_ref=buf.at[:, 0:8, :],
            send_sem=a_send.at[base], recv_sem=a_recv.at[base],
            device_id=(jnp.minimum(blk + 1, n_blk - 1), sub), device_id_type=MESH)
        left = pltpu.make_async_remote_copy(
            src_ref=buf.at[:, 8:16, :], dst_ref=buf.at[:, 264:272, :],
            send_sem=a_send.at[base + 1], recv_sem=a_recv.at[base + 1],
            device_id=(jnp.maximum(blk - 1, 0), sub), device_id_type=MESH)
        return right, left

    def start_a(buf, base):
        right, left = a_copies(buf, base)

        @pl.when(has_right)
        def _():
            right.start()

        @pl.when(has_left)
        def _():
            left.start()

    def wait_a_recv(buf, base):
        right, left = a_copies(buf, base)

        @pl.when(has_left)
        def _():
            right.wait_recv()

        @pl.when(has_right)
        def _():
            left.wait_recv()

    def wait_a_send(buf, base):
        right, left = a_copies(buf, base)

        @pl.when(has_right)
        def _():
            right.wait_send()

        @pl.when(has_left)
        def _():
            left.wait_send()

    n_copy0 = [
        pltpu.make_async_remote_copy(
            src_ref=nsend0.at[:, low:high], dst_ref=nrecv0.at[:, low:high],
            send_sem=n0_send.at[n], recv_sem=n0_recv.at[n], device_id=partner, device_id_type=MESH)
        for n, (low, high) in enumerate(GHOSTS)]
    n_copy0[0].start()
    start_a(psi0, 0)
    for copy in n_copy0[1:]:
        copy.start()

    loads[1].wait()
    loads[2].wait()
    table = slot_v[...]
    for g in range(4):
        patch = face_v[8 * g:8 * g + 8, :]
        lane, high = patch & 127, patch >> 7
        found = jnp.zeros((8, 128), jnp.int32)
        for j in range(16):
            line = jnp.broadcast_to(table[j:j + 1, :], (8, 128))
            found = jnp.where(high == j, jnp.take_along_axis(line, lane, axis=1), found)
        j_, sub_, core_ = found & 7, (found >> 3) & 1, (found >> 4) & 1
        z_, x_, yh_ = (found >> 5) & 7, (found >> 8) & 3, (found >> 10) & 1
        row = (core_ << 9) + (x_ << 7) + (z_ << 4) + (yh_ << 3) + j_
        key[8 * g:8 * g + 8, :] = jnp.where(sub_ == sub, row, -1)

    def fill(q, carry):
        k = jnp.broadcast_to(key[pl.ds(lax.rem(q + 2, 32), 1), :], (16, 128))
        same = (k & 15) == lax.broadcasted_iota(jnp.int32, (16, 128), 0)
        tile = jnp.where(jnp.logical_and(same, k >= 0), k >> 4, -1).astype(F32).astype(BF16)
        one, zero = jnp.ones((16, 128), BF16), jnp.zeros((16, 128), BF16)
        for m in range(64):
            onehot[16 * m:16 * m + 16, pl.ds(pl.multiple_of(q * 128, 128), 128)] = jnp.where(
                tile == jnp.array(m, BF16), one, zero)
        return carry

    def widen(a, carry):
        geom32[a] = geom[pl.ds(pl.multiple_of(a * 256, 256), 256), :].astype(F32)
        return carry

    sub_iota = lax.broadcasted_iota(jnp.int32, (16, 128), 0) & 7
    lane_iota = lax.broadcasted_iota(jnp.int32, (16, 128), 1)
    edge_n = jnp.where(
        sub == 0, jnp.where(sub_iota == 7, -1.0, 0.0), jnp.where(sub_iota == 0, 1.0, 0.0)).astype(F32)

    def sweep_pair(p, buf, halo, halo_row):
        rows = pl.ds(pl.multiple_of(16 * p, 16), 16)
        stab_acc, jac_acc, psi = [None] * NV, [None] * NV, [None] * NV

        def add(total, term):
            return term if total is None else total + term

        for u in range(NV):
            four = buf[u, pl.ds(pl.multiple_of(16 * p, 16), 32), :]
            here = four[8:24]
            psi[u] = here
            d_a = four[0:16] - four[16:32]
            before = jnp.concatenate([pltpu.roll(here[0:8], 1, 0), pltpu.roll(here[8:16], 1, 0)], 0)
            after = jnp.concatenate([pltpu.roll(here[0:8], 7, 0), pltpu.roll(here[8:16], 7, 0)], 0)
            ghost = jnp.concatenate([jnp.broadcast_to(halo[u, halo_row], (8, 128)),
                                     jnp.broadcast_to(halo[u, halo_row + 1], (8, 128))], 0)
            d_n = jnp.where(sub_iota == 0, 0.0, before) - jnp.where(sub_iota == 7, 0.0, after) + edge_n * ghost
            d_c = (jnp.where(lane_iota == 0, 0.0, pltpu.roll(here, 1, 1))
                   - jnp.where(lane_iota == 127, 0.0, pltpu.roll(here, 127, 1)))
            for v in range(NV):
                i = u * NV + v
                stab_acc[v] = add(stab_acc[v], stab[i, rows, :].astype(F32) * here)
                jac_acc[v] = add(jac_acc[v], jac[i, rows, :].astype(F32) * d_a)
                jac_acc[v] = jac_acc[v] + jac[25 + i, rows, :].astype(F32) * d_n
                jac_acc[v] = jac_acc[v] + jac[50 + i, rows, :].astype(F32) * d_c
        resid = [grad[v, rows, :] - stab_acc[v] - 0.5 * jac_acc[v] for v in range(NV)]
        result = []
        for u in range(NV):
            step = None
            for v in range(NV):
                step = add(step, prec[u * NV + v, rows, :].astype(F32) * resid[v])
            result.append(psi[u] + step)
        return result

    def n_copy1(d):
        part = pl.ds(4 * d, 4)
        return pltpu.make_async_remote_copy(
            src_ref=nsend1.at[:, part], dst_ref=nrecv1.at[:, part], send_sem=n_send.at[d], recv_sem=n_recv.at[d],
            device_id=partner, device_id_type=MESH)

    def first_part(s, carry):
        d = jnp.where(s < 2, s + 1, jnp.where(s == 2, 0, s))

        for n, step in enumerate((0, 2, 3, 6)):
            @pl.when(s == step)
            def _():
                for part in PART_OF[n]:
                    for load in parts[part]:
                        load.wait()
                n_copy0[n].wait_recv()
                if n == 1:
                    wait_a_recv(psi0, 0)

        def pair(j, carry):
            p = lax.rem(2 * d + j + 15, 16)
            row = 4 * d + 2 * j
            new = sweep_pair(p, psi0, nrecv0, row)
            for v in range(NV):
                psi1[v, pl.ds(pl.multiple_of(16 * p + 8, 8), 16), :] = new[v]
                nsend1[v, row] = edge_row(new[v][0:8])
                nsend1[v, row + 1] = edge_row(new[v][8:16])
            return carry

        lax.fori_loop(0, 2, pair, 0)
        n_copy1(d).start()

        @pl.when(s == 2)
        def _():
            start_a(psi1, 2)

        return carry

    lax.fori_loop(0, 8, first_part, 0)
    lax.fori_loop(0, 32, fill, 0)

    is_wall = core == sub
    not_wall = jnp.logical_not(is_wall)

    def s_copy(k):
        part = pl.ds(pl.multiple_of(8 * k, 8), 8)
        return pltpu.make_async_remote_copy(
            src_ref=sens_loc.at[:, part, :], dst_ref=sens.at[:, part, :], send_sem=s_send.at[k], recv_sem=s_recv.at[k],
            device_id=partner, device_id_type=MESH)

    def wall_row(plane):
        return jnp.where(sub == 0, plane[0:1], plane[7:8])

    loads[3].wait()

    def second_part(s, carry):
        d = lax.rem(s + 1, 8)
        n_copy1(d).wait_recv()

        @pl.when(s == 7)
        def _():
            wait_a_recv(psi1, 2)

        def pair(j, carry):
            p = lax.rem(2 * d + j + 15, 16)
            q = 4 * s + 2 * j
            new = sweep_pair(p, psi1, nrecv1, 4 * d + 2 * j)
            for v in range(NV):
                psi2[v, pl.ds(pl.multiple_of(16 * p, 16), 16), :] = new[v]
            for j in range(2):
                total = weight_s[j, 0] * new[0]
                for v in range(1, NV):
                    total = total + weight_s[j, v] * new[v]
                sens_loc[j, pl.ds(q, 1), :] = wall_row(total[0:8])
                sens_loc[j, pl.ds(q + 1, 1), :] = wall_row(total[8:16])
            return carry

        lax.fori_loop(0, 2, pair, 0)

        @pl.when(jnp.logical_and(is_wall, lax.rem(s, 2) == 1))
        def _():
            k = s // 2
            s_copy(k).start()
            part = pl.ds(pl.multiple_of(8 * k, 8), 8)
            sens[:, part, :] = sens_loc[:, part, :]

        return carry

    lax.fori_loop(0, 8, second_part, 0)
    state_copy = pltpu.make_async_copy(psi2, state_h, out_sem)
    state_copy.start()
    loads[4].wait()
    lax.fori_loop(0, 32, widen, 0)

    def make_contrib(k):
        @pl.when(not_wall)
        def _():
            s_copy(k).wait_recv()

        part = pl.ds(pl.multiple_of(8 * k, 8), 8)
        pressure = jnp.transpose(sens[0, part, :])
        shear = jnp.transpose(sens[1, part, :])
        for r in range(8):
            a = lax.rem(8 * k + 2 + r, 32)
            g0 = geom32[a, pl.ds(0, 128, 2), :]
            g1 = geom32[a, pl.ds(1, 128, 2), :]
            c = pressure[:, r:r + 1] * g0 + shear[:, r:r + 1] * g1
            hi = c.astype(BF16)
            lo = (c - hi.astype(F32)).astype(BF16)
            contrib[128 * r:128 * r + 128, 0:128] = hi
            contrib[128 * r:128 * r + 128, 128:256] = lo

    def product(row, k):
        part = onehot[pl.ds(pl.multiple_of(row, 512), 512), pl.ds(pl.multiple_of(k * 1024, 1024), 1024)]
        both = jnp.dot(part, contrib[...], preferred_element_type=F32)
        return both[:, 0:128] + both[:, 128:256]

    acc[...] = jnp.zeros((1024, 128), F32)

    def quarter(k, carry):
        make_contrib(k)

        def block(m, carry):
            rows = pl.ds(pl.multiple_of(m * 512, 512), 512)
            acc[rows, :] += product(m * 512, k)
            return carry

        lax.fori_loop(0, 2, block, 0)
        return carry

    lax.fori_loop(0, 3, quarter, 0)
    make_contrib(3)

    def order(k):
        return jnp.where(k == 0, 2, jnp.where(k == 1, 3, 3 - k)) if not isinstance(k, int) else (2, 3, 1, 0)[k]

    def c_copy(k):
        start = (1 - core) * 512 + lax.rem(x + order(k), NX) * 128
        return pltpu.make_async_remote_copy(
            src_ref=acc.at[pl.ds(pl.multiple_of(start, 128), 128), :], dst_ref=core_in.at[k],
            send_sem=c_send.at[k], recv_sem=c_recv.at[k], device_id=core_peer, device_id_type=MESH)

    def x_copy(k):
        peer = (at(yh, lax.rem(x + order(k), NX), z, core), sub)
        return pltpu.make_async_remote_copy(
            src_ref=x_out.at[k], dst_ref=x_in.at[k],
            send_sem=x_send.at[k], recv_sem=x_recv.at[k], device_id=peer, device_id_type=MESH)

    rows = pl.ds(pl.multiple_of((1 - core) * 512, 512), 512)
    acc[rows, :] += product((1 - core) * 512, 3)
    for k in range(4):
        c_copy(k).start()
    rows = pl.ds(pl.multiple_of(core * 512, 512), 512)
    acc[rows, :] += product(core * 512, 3)

    def kept(k, carry):
        start = core * 512 + lax.rem(x + order(k), NX) * 128
        c_copy(k).wait_recv()
        x_out[k] = acc[pl.ds(pl.multiple_of(start, 128), 128), :] + core_in[k]

        @pl.when(order(k) != 0)
        def _():
            x_copy(k).start()

        return carry

    lax.fori_loop(0, 4, kept, 0)
    for k in (1, 2, 0):
        x_copy(k).wait_recv()
    z_out[...] = x_out[3] + x_in[0] + x_in[1] + x_in[2]

    def z_copy(d):
        dest = lax.rem(z + d, NZ)
        peer = (at(yh, x, dest, core), sub)
        return pltpu.make_async_remote_copy(
            src_ref=z_out.at[pl.ds(pl.multiple_of(dest * 16, 16), 16), :], dst_ref=z_in.at[d - 1],
            send_sem=z_send.at[d - 1], recv_sem=z_recv.at[d - 1], device_id=peer, device_id_type=MESH)

    for d in (4, 3, 5, 2, 6, 1, 7):
        z_copy(d).start()
    for d in range(1, NZ):
        z_copy(d).wait_recv()
    total = z_out[pl.ds(pl.multiple_of(z * 16, 16), 16), :]
    for d in range(NZ - 1):
        total = total + z_in[d]
    y_out[...] = total

    y_rows = [1 - yh, 1 - yh, yh]

    def y_copy(k):
        return pltpu.make_async_remote_copy(
            src_ref=y_out.at[pl.ds(pl.multiple_of(y_rows[k] * 8, 8), 8), :], dst_ref=y_in.at[k],
            send_sem=y_send.at[k], recv_sem=y_recv.at[k], device_id=y_peer[k], device_id_type=MESH)

    for k in range(3):
        y_copy(k).start()
    for k in range(3):
        y_copy(k).wait_recv()
    mine = pl.ds(pl.multiple_of(8 * sub, 8), 8)
    others = pl.ds(pl.multiple_of(8 * (1 - sub), 8), 8)
    patch_v[mine, :] = y_out[pl.ds(pl.multiple_of(yh * 8, 8), 8), :] + y_in[0]
    patch_v[others, :] = y_in[1] + y_in[2]

    for copy in n_copy0:
        copy.wait_send()
    wait_a_send(psi0, 0)
    wait_a_send(psi1, 2)
    for d in range(8):
        n_copy1(d).wait_send()

    @pl.when(is_wall)
    def _():
        for k in range(4):
            s_copy(k).wait_send()

    for k in range(4):
        c_copy(k).wait_send()
    for k in range(3):
        x_copy(k).wait_send()
    for d in range(1, NZ):
        z_copy(d).wait_send()
    for k in range(3):
        y_copy(k).wait_send()
    state_copy.wait()


def hand_on(state_in, patch_in, state_out, patch_out, state, patch, in_sem, out_sem):
    pieces = [(patch_in, patch, patch_out)] + [(state_in.at[v], state.at[v], state_out.at[v]) for v in range(NV)]
    enter = [pltpu.make_async_copy(a, b, in_sem.at[n]) for n, (a, b, _) in enumerate(pieces)]
    leave = [pltpu.make_async_copy(b, c, out_sem.at[n]) for n, (_, b, c) in enumerate(pieces)]
    for copy in enter:
        copy.start()
    for n, copy in enumerate(enter):
        copy.wait()
        leave[n].start()
    for copy in leave:
        copy.wait()


def local(
    adjoint_start, objective_grad, flux_jacobian, stab_block, precond_block,
    wall_weight, wall_geometry, face_patch, patch_slot,
):
    any_, vmem = (pl.BlockSpec(memory_space=m) for m in (pl.ANY, pltpu.VMEM))
    dma = pltpu.SemaphoreType.DMA
    state, patch = pl.pallas_call(
        kernel,
        out_shape=(jax.ShapeDtypeStruct((NV, 256, 128), F32), jax.ShapeDtypeStruct((16, 128), F32)),
        in_specs=[any_] * 9,
        out_specs=(any_, vmem),
        scratch_shapes=[
            pltpu.VMEM((NV, 272, 128), F32),
            pltpu.VMEM((NV, 272, 128), F32),
            pltpu.VMEM((NV, 256, 128), F32),
            pltpu.VMEM((NV, 256, 128), F32),
            pltpu.VMEM((75, 256, 128), BF16),
            pltpu.VMEM((25, 256, 128), BF16),
            pltpu.VMEM((25, 256, 128), BF16),
            pltpu.VMEM((8192, 128), BF16),
            pltpu.SMEM((2, NV), F32),
            pltpu.VMEM((32, 128), jnp.int32),
            pltpu.VMEM((16, 128), jnp.int32),
            pltpu.VMEM((32, 256, 128), F32),
            pltpu.VMEM((1024, 4096), BF16),
            pltpu.VMEM((32, 128), jnp.int32),
            pltpu.VMEM((1024, 256), BF16),
            pltpu.VMEM((1024, 128), F32),
            pltpu.VMEM((NV, 32, 1, 128), F32),
            pltpu.VMEM((NV, 32, 1, 128), F32),
            pltpu.VMEM((NV, 32, 1, 128), F32),
            pltpu.VMEM((NV, 32, 1, 128), F32),
            pltpu.VMEM((2, 32, 128), F32),
            pltpu.VMEM((2, 32, 128), F32),
            pltpu.VMEM((4, 128, 128), F32),
            pltpu.VMEM((4, 128, 128), F32),
            pltpu.VMEM((4, 128, 128), F32),
            pltpu.VMEM((128, 128), F32),
            pltpu.VMEM((NZ - 1, 16, 128), F32),
            pltpu.VMEM((16, 128), F32),
            pltpu.VMEM((3, 8, 128), F32),
            dma((5,)), dma((4 * len(PARTS),)), dma,
            dma((4,)), dma((4,)),
            dma((4,)), dma((4,)), dma((8,)), dma((8,)),
            dma((4,)), dma((4,)),
            dma((4,)), dma((4,)),
            dma((4,)), dma((4,)),
            dma((NZ - 1,)), dma((NZ - 1,)),
            dma((3,)), dma((3,)),
        ],
        compiler_params=pltpu.CompilerParams(
            collective_id=0, has_side_effects=True, vmem_limit_bytes=60 * 1024 * 1024),
    )(
        adjoint_start.reshape(NV, 256, 128),
        objective_grad.reshape(NV, 256, 128),
        flux_jacobian.reshape(75, 256, 128),
        stab_block.reshape(25, 256, 128),
        precond_block.reshape(25, 256, 128),
        wall_weight.T,
        wall_geometry.reshape(8192, 128),
        face_patch.reshape(32, 128),
        patch_slot.reshape(16, 128),
    )
    state, patch = pl.pallas_call(
        hand_on,
        out_shape=(jax.ShapeDtypeStruct(state.shape, F32), jax.ShapeDtypeStruct(patch.shape, F32)),
        in_specs=[any_, any_],
        out_specs=(any_, any_),
        scratch_shapes=[pltpu.VMEM((NV, 256, 128), F32), pltpu.VMEM((16, 128), F32), dma((6,)), dma((6,))],
        compiler_params=pltpu.CompilerParams(vmem_limit_bytes=60 * 1024 * 1024),
    )(state, patch)
    return state.reshape(NV, 32, 8, 128), patch


def solution(mesh):
    return jax.shard_map(
        local,
        mesh=mesh,
        in_specs=(
            P(None, "blk", "sub", None),
            P(None, "blk", "sub", None),
            P(None, None, None, "blk", "sub", None),
            P(None, None, "blk", "sub", None),
            P(None, None, "blk", "sub", None),
            P(),
            P("blk", None, None),
            P("blk"),
            P(),
        ),
        out_specs=(P(None, "blk", "sub", None), P("blk", None)),
        check_vma=False,
    )
```

```python
import functools

import jax
import jax.numpy as jnp
from jax import lax
from jax.experimental import pallas as pl
from jax.experimental.pallas import tpu as pltpu
from jax.sharding import PartitionSpec as P

MESH = pl.DeviceIdType.MESH
F32 = jnp.float32
BF16 = jnp.bfloat16

NV = 5
PARTS = ((16, 80), (0, 16), (240, 256), (80, 176), (176, 240))
PART_OF = ((0,), (1, 2), (3,), (4,))
GHOSTS = ((4, 12), (0, 4), (12, 24), (24, 32))
NX, NZ = 4, 8


def kernel(
    start_h, grad_h, jac_h, stab_h, prec_h, weight_h, geom_h, face_h, slot_h,
    state_h, patch_v,
    psi0, psi1, psi2, grad, jac, stab, prec, geom, weight_s, face_v, slot_v, geom32, onehot, key, contrib, acc,
    nsend0, nrecv0, nsend1, nrecv1, sens_loc, sens,
    core_in, ax_out, ax_in, az_out, az_in, bz_out, bz_in, bx_out, bx_in, y_out, y_in,
    load_sem, part_sem, out_sem, a_send, a_recv, n0_send, n0_recv, n_send, n_recv, s_send, s_recv,
    c_send, c_recv, ax_send, ax_recv, az_send, az_recv, bz_send, bz_recv, bx_send, bx_recv, y_send, y_recv,
):
    blk, sub = lax.axis_index("blk"), lax.axis_index("sub")
    n_blk = lax.axis_size("blk")
    core = lax.rem(blk, 2)
    z = lax.rem(blk // 2, NZ)
    x = lax.rem(blk // (2 * NZ), NX)
    yh = blk // (2 * NZ * NX)

    def at(yh_, x_, z_, core_):
        return ((yh_ * NX + x_) * NZ + z_) * 2 + core_

    core_peer = (at(yh, x, z, 1 - core), sub)
    x_peer = [(at(yh, lax.rem(x + d, NX), z, core), sub) for d in range(NX)]
    z_peer = [(at(yh, x, lax.rem(z + d, NZ), core), sub) for d in range(NZ)]
    y_peer = [(at(1 - yh, x, z, core), sub), (at(1 - yh, x, z, core), 1 - sub), (blk, 1 - sub)]
    partner = (blk, 1 - sub)
    has_left, has_right = blk > 0, blk < n_blk - 1
    other = jnp.where(core == 1, blk + 1, blk - 1)
    has_other = jnp.logical_and(other >= 0, other < n_blk)

    barrier = pltpu.get_barrier_semaphore()
    peers = [core_peer] + x_peer[1:] + z_peer[1:] + y_peer
    for peer in peers:
        pl.semaphore_signal(barrier, inc=1, device_id=peer, device_id_type=MESH)

    @pl.when(has_other)
    def _():
        pl.semaphore_signal(barrier, inc=1, device_id=(other, sub), device_id_type=MESH)

    loads = [
        pltpu.make_async_copy(start_h, psi0.at[:, 8:264, :], load_sem.at[0]),
        pltpu.make_async_copy(face_h, face_v, load_sem.at[1]),
        pltpu.make_async_copy(slot_h, slot_v, load_sem.at[2]),
        pltpu.make_async_copy(weight_h, weight_s, load_sem.at[3]),
        pltpu.make_async_copy(geom_h, geom, load_sem.at[4]),
    ]
    parts = []
    for n, (low, high) in enumerate(PARTS):
        rows = slice(low, high)
        parts.append([
            pltpu.make_async_copy(far.at[:, rows, :], near.at[:, rows, :], part_sem.at[4 * n + j])
            for j, (far, near) in enumerate(((jac_h, jac), (stab_h, stab), (prec_h, prec), (grad_h, grad)))
        ])
    for load in loads[:4]:
        load.start()
    for part in parts:
        for load in part:
            load.start(priority=1)
    loads[4].start(priority=1)

    zero_plane = jnp.zeros((NV, 8, 128), F32)
    for buf in (psi0, psi1):
        @pl.when(jnp.logical_not(has_left))
        def _():
            buf[:, 0:8, :] = zero_plane

        @pl.when(jnp.logical_not(has_right))
        def _():
            buf[:, 264:272, :] = zero_plane

    loads[0].wait()

    def edge_row(plane):
        return jnp.where(sub == 0, plane[7:8], plane[0:1])

    def pick0(q, carry):
        a = lax.rem(q + 30, 32)
        for v in range(NV):
            nsend0[v, q] = edge_row(psi0[v, pl.ds(pl.multiple_of(8 * a + 8, 8), 8), :])
        return carry

    lax.fori_loop(0, 32, pick0, 0)

    pl.semaphore_wait(barrier, len(peers) + has_other.astype(jnp.int32))

    def a_copies(buf, base):
        right = pltpu.make_async_remote_copy(
            src_ref=buf.at[:, 256:264, :], dst_ref=buf.at[:, 0:8, :],
            send_sem=a_send.at[base], recv_sem=a_recv.at[base],
            device_id=(jnp.minimum(blk + 1, n_blk - 1), sub), device_id_type=MESH)
        left = pltpu.make_async_remote_copy(
            src_ref=buf.at[:, 8:16, :], dst_ref=buf.at[:, 264:272, :],
            send_sem=a_send.at[base + 1], recv_sem=a_recv.at[base + 1],
            device_id=(jnp.maximum(blk - 1, 0), sub), device_id_type=MESH)
        return right, left

    def start_a(buf, base):
        right, left = a_copies(buf, base)

        @pl.when(has_right)
        def _():
            right.start()

        @pl.when(has_left)
        def _():
            left.start()

    def wait_a_recv(buf, base):
        right, left = a_copies(buf, base)

        @pl.when(has_left)
        def _():
            right.wait_recv()

        @pl.when(has_right)
        def _():
            left.wait_recv()

    def wait_a_send(buf, base):
        right, left = a_copies(buf, base)

        @pl.when(has_right)
        def _():
            right.wait_send()

        @pl.when(has_left)
        def _():
            left.wait_send()

    n_copy0 = [
        pltpu.make_async_remote_copy(
            src_ref=nsend0.at[:, low:high], dst_ref=nrecv0.at[:, low:high],
            send_sem=n0_send.at[n], recv_sem=n0_recv.at[n], device_id=partner, device_id_type=MESH)
        for n, (low, high) in enumerate(GHOSTS)]
    n_copy0[0].start()
    start_a(psi0, 0)
    for copy in n_copy0[1:]:
        copy.start()

    loads[1].wait()
    loads[2].wait()
    table = slot_v[...]
    for g in range(4):
        patch = face_v[8 * g:8 * g + 8, :]
        lane, high = patch & 127, patch >> 7
        found = jnp.zeros((8, 128), jnp.int32)
        for j in range(16):
            line = jnp.broadcast_to(table[j:j + 1, :], (8, 128))
            found = jnp.where(high == j, jnp.take_along_axis(line, lane, axis=1), found)
        j_, sub_, core_ = found & 7, (found >> 3) & 1, (found >> 4) & 1
        z_, x_, yh_ = (found >> 5) & 7, (found >> 8) & 3, (found >> 10) & 1
        place = jnp.where(yh_ == 0, (x_ << 6) + (z_ << 3), (z_ << 5) + (x_ << 3))
        row = (core_ << 9) + (yh_ << 8) + place + j_
        key[8 * g:8 * g + 8, :] = jnp.where(sub_ == sub, row, -1)

    def fill(q, carry):
        k = jnp.broadcast_to(key[pl.ds(lax.rem(q + 2, 32), 1), :], (16, 128))
        same = (k & 15) == lax.broadcasted_iota(jnp.int32, (16, 128), 0)
        tile = jnp.where(jnp.logical_and(same, k >= 0), k >> 4, -1).astype(F32).astype(BF16)
        one, zero = jnp.ones((16, 128), BF16), jnp.zeros((16, 128), BF16)
        for m in range(64):
            onehot[16 * m:16 * m + 16, pl.ds(pl.multiple_of(q * 128, 128), 128)] = jnp.where(
                tile == jnp.array(m, BF16), one, zero)
        return carry

    def widen(a, carry):
        geom32[a] = geom[pl.ds(pl.multiple_of(a * 256, 256), 256), :].astype(F32)
        return carry

    sub_iota = lax.broadcasted_iota(jnp.int32, (16, 128), 0) & 7
    lane_iota = lax.broadcasted_iota(jnp.int32, (16, 128), 1)
    edge_n = jnp.where(
        sub == 0, jnp.where(sub_iota == 7, -1.0, 0.0), jnp.where(sub_iota == 0, 1.0, 0.0)).astype(F32)

    def sweep_pair(p, buf, halo, halo_row):
        rows = pl.ds(pl.multiple_of(16 * p, 16), 16)
        stab_acc, jac_acc, psi = [None] * NV, [None] * NV, [None] * NV

        def add(total, term):
            return term if total is None else total + term

        for u in range(NV):
            four = buf[u, pl.ds(pl.multiple_of(16 * p, 16), 32), :]
            here = four[8:24]
            psi[u] = here
            d_a = four[0:16] - four[16:32]
            before = jnp.concatenate([pltpu.roll(here[0:8], 1, 0), pltpu.roll(here[8:16], 1, 0)], 0)
            after = jnp.concatenate([pltpu.roll(here[0:8], 7, 0), pltpu.roll(here[8:16], 7, 0)], 0)
            ghost = jnp.concatenate([jnp.broadcast_to(halo[u, halo_row], (8, 128)),
                                     jnp.broadcast_to(halo[u, halo_row + 1], (8, 128))], 0)
            d_n = jnp.where(sub_iota == 0, 0.0, before) - jnp.where(sub_iota == 7, 0.0, after) + edge_n * ghost
            d_c = (jnp.where(lane_iota == 0, 0.0, pltpu.roll(here, 1, 1))
                   - jnp.where(lane_iota == 127, 0.0, pltpu.roll(here, 127, 1)))
            for v in range(NV):
                i = u * NV + v
                stab_acc[v] = add(stab_acc[v], stab[i, rows, :].astype(F32) * here)
                jac_acc[v] = add(jac_acc[v], jac[i, rows, :].astype(F32) * d_a)
                jac_acc[v] = jac_acc[v] + jac[25 + i, rows, :].astype(F32) * d_n
                jac_acc[v] = jac_acc[v] + jac[50 + i, rows, :].astype(F32) * d_c
        resid = [grad[v, rows, :] - stab_acc[v] - 0.5 * jac_acc[v] for v in range(NV)]
        result = []
        for u in range(NV):
            step = None
            for v in range(NV):
                step = add(step, prec[u * NV + v, rows, :].astype(F32) * resid[v])
            result.append(psi[u] + step)
        return result

    def n_copy1(d):
        part = pl.ds(4 * d, 4)
        return pltpu.make_async_remote_copy(
            src_ref=nsend1.at[:, part], dst_ref=nrecv1.at[:, part], send_sem=n_send.at[d], recv_sem=n_recv.at[d],
            device_id=partner, device_id_type=MESH)

    def first_part(s, carry):
        d = jnp.where(s < 2, s + 1, jnp.where(s == 2, 0, s))

        for n, step in enumerate((0, 2, 3, 6)):
            @pl.when(s == step)
            def _():
                for part in PART_OF[n]:
                    for load in parts[part]:
                        load.wait()
                n_copy0[n].wait_recv()
                if n == 1:
                    wait_a_recv(psi0, 0)

        def pair(j, carry):
            p = lax.rem(2 * d + j + 15, 16)
            row = 4 * d + 2 * j
            new = sweep_pair(p, psi0, nrecv0, row)
            for v in range(NV):
                psi1[v, pl.ds(pl.multiple_of(16 * p + 8, 8), 16), :] = new[v]
                nsend1[v, row] = edge_row(new[v][0:8])
                nsend1[v, row + 1] = edge_row(new[v][8:16])
            return carry

        lax.fori_loop(0, 2, pair, 0)
        n_copy1(d).start()

        @pl.when(s == 2)
        def _():
            start_a(psi1, 2)

        return carry

    lax.fori_loop(0, 8, first_part, 0)
    lax.fori_loop(0, 32, fill, 0)

    is_wall = core == sub
    not_wall = jnp.logical_not(is_wall)

    def s_copy(k):
        part = pl.ds(pl.multiple_of(8 * k, 8), 8)
        return pltpu.make_async_remote_copy(
            src_ref=sens_loc.at[:, part, :], dst_ref=sens.at[:, part, :], send_sem=s_send.at[k], recv_sem=s_recv.at[k],
            device_id=partner, device_id_type=MESH)

    def wall_row(plane):
        return jnp.where(sub == 0, plane[0:1], plane[7:8])

    loads[3].wait()

    def second_part(s, carry):
        d = lax.rem(s + 1, 8)
        n_copy1(d).wait_recv()

        @pl.when(s == 7)
        def _():
            wait_a_recv(psi1, 2)

        def pair(j, carry):
            p = lax.rem(2 * d + j + 15, 16)
            q = 4 * s + 2 * j
            new = sweep_pair(p, psi1, nrecv1, 4 * d + 2 * j)
            for v in range(NV):
                psi2[v, pl.ds(pl.multiple_of(16 * p, 16), 16), :] = new[v]
            for j in range(2):
                total = weight_s[j, 0] * new[0]
                for v in range(1, NV):
                    total = total + weight_s[j, v] * new[v]
                sens_loc[j, pl.ds(q, 1), :] = wall_row(total[0:8])
                sens_loc[j, pl.ds(q + 1, 1), :] = wall_row(total[8:16])
            return carry

        lax.fori_loop(0, 2, pair, 0)

        @pl.when(jnp.logical_and(is_wall, lax.rem(s, 2) == 1))
        def _():
            k = s // 2
            s_copy(k).start()
            part = pl.ds(pl.multiple_of(8 * k, 8), 8)
            sens[:, part, :] = sens_loc[:, part, :]

        return carry

    lax.fori_loop(0, 8, second_part, 0)
    state_copy = pltpu.make_async_copy(psi2, state_h, out_sem)
    state_copy.start()
    loads[4].wait()
    lax.fori_loop(0, 32, widen, 0)

    def make_contrib(k):
        @pl.when(not_wall)
        def _():
            s_copy(k).wait_recv()

        part = pl.ds(pl.multiple_of(8 * k, 8), 8)
        pressure = jnp.transpose(sens[0, part, :])
        shear = jnp.transpose(sens[1, part, :])
        for r in range(8):
            a = lax.rem(8 * k + 2 + r, 32)
            g0 = geom32[a, pl.ds(0, 128, 2), :]
            g1 = geom32[a, pl.ds(1, 128, 2), :]
            c = pressure[:, r:r + 1] * g0 + shear[:, r:r + 1] * g1
            hi = c.astype(BF16)
            lo = (c - hi.astype(F32)).astype(BF16)
            contrib[128 * r:128 * r + 128, 0:128] = hi
            contrib[128 * r:128 * r + 128, 128:256] = lo

    def product(row, rows, k):
        part = onehot[pl.ds(pl.multiple_of(row, 512), rows), pl.ds(pl.multiple_of(k * 1024, 1024), 1024)]
        both = jnp.dot(part, contrib[...], preferred_element_type=F32)
        return both[:, 0:128] + both[:, 128:256]

    acc[...] = jnp.zeros((1024, 128), F32)

    def quarter(k, carry):
        make_contrib(k)
        acc[...] += product(0, 1024, k)
        return carry

    lax.fori_loop(0, 3, quarter, 0)
    make_contrib(3)

    def c_copy(h):
        return pltpu.make_async_remote_copy(
            src_ref=acc.at[pl.ds(pl.multiple_of((1 - core) * 512 + h * 256, 256), 256), :], dst_ref=core_in.at[h],
            send_sem=c_send.at[h], recv_sem=c_recv.at[h], device_id=core_peer, device_id_type=MESH)

    def spread(out, into, send, recv, peer, place, size):
        def copy(d):
            dest = lax.rem(place + d, size)
            rows = out.shape[0] // size
            return pltpu.make_async_remote_copy(
                src_ref=out.at[pl.ds(pl.multiple_of(dest * rows, rows), rows), :], dst_ref=into.at[d - 1],
                send_sem=send.at[d - 1], recv_sem=recv.at[d - 1], device_id=peer[d], device_id_type=MESH)
        return copy

    ax_copy = spread(ax_out, ax_in, ax_send, ax_recv, x_peer, x, NX)
    az_copy = spread(az_out, az_in, az_send, az_recv, z_peer, z, NZ)
    bz_copy = spread(bz_out, bz_in, bz_send, bz_recv, z_peer, z, NZ)
    bx_copy = spread(bx_out, bx_in, bx_send, bx_recv, x_peer, x, NX)
    x_order, z_order = (2, 3, 1), (4, 3, 5, 2, 6, 1, 7)

    def gathered(out, into, copy, place, size):
        rows = out.shape[0] // size
        for d in range(1, size):
            copy(d).wait_recv()
        total = out[pl.ds(pl.multiple_of(place * rows, rows), rows), :]
        for d in range(1, size):
            total = total + into[d - 1]
        return total

    acc[pl.ds(pl.multiple_of((1 - core) * 512, 512), 512), :] += product((1 - core) * 512, 512, 3)
    for h in (1, 0):
        c_copy(h).start()
    acc[pl.ds(pl.multiple_of(core * 512, 512), 512), :] += product(core * 512, 512, 3)

    c_copy(1).wait_recv()
    bz_out[...] = acc[pl.ds(pl.multiple_of(core * 512 + 256, 256), 256), :] + core_in[1]
    for d in z_order:
        bz_copy(d).start()
    c_copy(0).wait_recv()
    ax_out[...] = acc[pl.ds(pl.multiple_of(core * 512, 256), 256), :] + core_in[0]
    for d in x_order:
        ax_copy(d).start()
    az_out[...] = gathered(ax_out, ax_in, ax_copy, x, NX)
    for d in z_order:
        az_copy(d).start()
    bx_out[...] = gathered(bz_out, bz_in, bz_copy, z, NZ)
    for d in x_order:
        bx_copy(d).start()
    y_out[8:16, :] = gathered(bx_out, bx_in, bx_copy, x, NX)
    y_out[0:8, :] = gathered(az_out, az_in, az_copy, z, NZ)

    y_rows = [1 - yh, 1 - yh, yh]

    def y_copy(k):
        return pltpu.make_async_remote_copy(
            src_ref=y_out.at[pl.ds(pl.multiple_of(y_rows[k] * 8, 8), 8), :], dst_ref=y_in.at[k],
            send_sem=y_send.at[k], recv_sem=y_recv.at[k], device_id=y_peer[k], device_id_type=MESH)

    for k in range(3):
        y_copy(k).start()
    for k in range(3):
        y_copy(k).wait_recv()
    mine = pl.ds(pl.multiple_of(8 * sub, 8), 8)
    others = pl.ds(pl.multiple_of(8 * (1 - sub), 8), 8)
    patch_v[mine, :] = y_out[pl.ds(pl.multiple_of(yh * 8, 8), 8), :] + y_in[0]
    patch_v[others, :] = y_in[1] + y_in[2]

    for copy in n_copy0:
        copy.wait_send()
    wait_a_send(psi0, 0)
    wait_a_send(psi1, 2)
    for d in range(8):
        n_copy1(d).wait_send()

    @pl.when(is_wall)
    def _():
        for k in range(4):
            s_copy(k).wait_send()

    for h in range(2):
        c_copy(h).wait_send()
    for d in range(1, NX):
        ax_copy(d).wait_send()
        bx_copy(d).wait_send()
    for d in range(1, NZ):
        az_copy(d).wait_send()
        bz_copy(d).wait_send()
    for k in range(3):
        y_copy(k).wait_send()
    state_copy.wait()


def hand_on(state_in, patch_in, state_out, patch_out, state, patch, in_sem, out_sem):
    pieces = [(patch_in, patch, patch_out)] + [(state_in.at[v], state.at[v], state_out.at[v]) for v in range(NV)]
    enter = [pltpu.make_async_copy(a, b, in_sem.at[n]) for n, (a, b, _) in enumerate(pieces)]
    leave = [pltpu.make_async_copy(b, c, out_sem.at[n]) for n, (_, b, c) in enumerate(pieces)]
    for copy in enter:
        copy.start()
    for n, copy in enumerate(enter):
        copy.wait()
        leave[n].start()
    for copy in leave:
        copy.wait()


def local(
    adjoint_start, objective_grad, flux_jacobian, stab_block, precond_block,
    wall_weight, wall_geometry, face_patch, patch_slot,
):
    any_, vmem = (pl.BlockSpec(memory_space=m) for m in (pl.ANY, pltpu.VMEM))
    dma = pltpu.SemaphoreType.DMA
    state, patch = pl.pallas_call(
        kernel,
        out_shape=(jax.ShapeDtypeStruct((NV, 256, 128), F32), jax.ShapeDtypeStruct((16, 128), F32)),
        in_specs=[any_] * 9,
        out_specs=(any_, vmem),
        scratch_shapes=[
            pltpu.VMEM((NV, 272, 128), F32),
            pltpu.VMEM((NV, 272, 128), F32),
            pltpu.VMEM((NV, 256, 128), F32),
            pltpu.VMEM((NV, 256, 128), F32),
            pltpu.VMEM((75, 256, 128), BF16),
            pltpu.VMEM((25, 256, 128), BF16),
            pltpu.VMEM((25, 256, 128), BF16),
            pltpu.VMEM((8192, 128), BF16),
            pltpu.SMEM((2, NV), F32),
            pltpu.VMEM((32, 128), jnp.int32),
            pltpu.VMEM((16, 128), jnp.int32),
            pltpu.VMEM((32, 256, 128), F32),
            pltpu.VMEM((1024, 4096), BF16),
            pltpu.VMEM((32, 128), jnp.int32),
            pltpu.VMEM((1024, 256), BF16),
            pltpu.VMEM((1024, 128), F32),
            pltpu.VMEM((NV, 32, 1, 128), F32),
            pltpu.VMEM((NV, 32, 1, 128), F32),
            pltpu.VMEM((NV, 32, 1, 128), F32),
            pltpu.VMEM((NV, 32, 1, 128), F32),
            pltpu.VMEM((2, 32, 128), F32),
            pltpu.VMEM((2, 32, 128), F32),
            pltpu.VMEM((2, 256, 128), F32),
            pltpu.VMEM((256, 128), F32),
            pltpu.VMEM((NX - 1, 64, 128), F32),
            pltpu.VMEM((64, 128), F32),
            pltpu.VMEM((NZ - 1, 8, 128), F32),
            pltpu.VMEM((256, 128), F32),
            pltpu.VMEM((NZ - 1, 32, 128), F32),
            pltpu.VMEM((32, 128), F32),
            pltpu.VMEM((NX - 1, 8, 128), F32),
            pltpu.VMEM((16, 128), F32),
            pltpu.VMEM((3, 8, 128), F32),
            dma((5,)), dma((4 * len(PARTS),)), dma,
            dma((4,)), dma((4,)),
            dma((4,)), dma((4,)), dma((8,)), dma((8,)),
            dma((4,)), dma((4,)),
            dma((2,)), dma((2,)),
            dma((NX - 1,)), dma((NX - 1,)), dma((NZ - 1,)), dma((NZ - 1,)),
            dma((NZ - 1,)), dma((NZ - 1,)), dma((NX - 1,)), dma((NX - 1,)),
            dma((3,)), dma((3,)),
        ],
        compiler_params=pltpu.CompilerParams(
            collective_id=0, has_side_effects=True, vmem_limit_bytes=60 * 1024 * 1024),
    )(
        adjoint_start.reshape(NV, 256, 128),
        objective_grad.reshape(NV, 256, 128),
        flux_jacobian.reshape(75, 256, 128),
        stab_block.reshape(25, 256, 128),
        precond_block.reshape(25, 256, 128),
        wall_weight.T,
        wall_geometry.reshape(8192, 128),
        face_patch.reshape(32, 128),
        patch_slot.reshape(16, 128),
    )
    state, patch = pl.pallas_call(
        hand_on,
        out_shape=(jax.ShapeDtypeStruct(state.shape, F32), jax.ShapeDtypeStruct(patch.shape, F32)),
        in_specs=[any_, any_],
        out_specs=(any_, any_),
        scratch_shapes=[pltpu.VMEM((NV, 256, 128), F32), pltpu.VMEM((16, 128), F32), dma((6,)), dma((6,))],
        compiler_params=pltpu.CompilerParams(vmem_limit_bytes=60 * 1024 * 1024),
    )(state, patch)
    return state.reshape(NV, 32, 8, 128), patch


def solution(mesh):
    return jax.shard_map(
        local,
        mesh=mesh,
        in_specs=(
            P(None, "blk", "sub", None),
            P(None, "blk", "sub", None),
            P(None, None, None, "blk", "sub", None),
            P(None, None, "blk", "sub", None),
            P(None, None, "blk", "sub", None),
            P(),
            P("blk", None, None),
            P("blk"),
            P(),
        ),
        out_specs=(P(None, "blk", "sub", None), P("blk", None)),
        check_vma=False,
    )
```

```python
import functools

import jax
import jax.numpy as jnp
from jax import lax
from jax.experimental import pallas as pl
from jax.experimental.pallas import tpu as pltpu
from jax.sharding import PartitionSpec as P

MESH = pl.DeviceIdType.MESH
F32 = jnp.float32
BF16 = jnp.bfloat16

NV = 5
PARTS = ((16, 80), (0, 16), (240, 256), (80, 176), (176, 240))
PART_OF = ((0,), (1, 2), (3,), (4,))
GHOSTS = ((4, 12), (0, 4), (12, 24), (24, 32))
NX, NZ = 4, 8


def kernel(
    start_h, grad_h, jac_h, stab_h, prec_h, weight_h, geom_h, face_h, slot_h,
    state_h, patch_v,
    psi0, psi1, psi2, grad, jac, stab, prec, geom, weight_s, face_v, slot_v, geom32, onehot, key, contrib, acc,
    nsend0, nrecv0, nsend1, nrecv1, sens_loc, sens,
    core_in, ax_out, ax_in, az_out, az_in, bz_out, bz_in, bx_out, bx_in, y_out, y_in,
    rounds, load_sem, part_sem, out_sem, a_send, a_recv, n0_send, n0_recv, n_send, n_recv, s_send, s_recv,
    c_send, c_recv, ax_send, ax_recv, az_send, az_recv, bz_send, bz_recv, bx_send, bx_recv, y_send, y_recv,
):
    blk, sub = lax.axis_index("blk"), lax.axis_index("sub")
    n_blk = lax.axis_size("blk")
    core = lax.rem(blk, 2)
    z = lax.rem(blk // 2, NZ)
    x = lax.rem(blk // (2 * NZ), NX)
    yh = blk // (2 * NZ * NX)

    def at(yh_, x_, z_, core_):
        return ((yh_ * NX + x_) * NZ + z_) * 2 + core_

    core_peer = (at(yh, x, z, 1 - core), sub)
    x_peer = [(at(yh, lax.rem(x + d, NX), z, core), sub) for d in range(NX)]
    z_peer = [(at(yh, x, lax.rem(z + d, NZ), core), sub) for d in range(NZ)]
    y_peer = [(at(1 - yh, x, z, core), sub), (at(1 - yh, x, z, core), 1 - sub), (blk, 1 - sub)]
    partner = (blk, 1 - sub)
    has_left, has_right = blk > 0, blk < n_blk - 1
    other = jnp.where(core == 1, blk + 1, blk - 1)
    has_other = jnp.logical_and(other >= 0, other < n_blk)

    barrier = pltpu.get_barrier_semaphore()
    near_z, near_x = [z_peer[1], z_peer[NZ - 1]], [x_peer[1], x_peer[NX - 1]]
    peers = [core_peer, y_peer[1], partner] + near_x + near_z
    for peer in peers:
        pl.semaphore_signal(barrier, inc=1, device_id=peer, device_id_type=MESH)

    @pl.when(has_other)
    def _():
        pl.semaphore_signal(barrier, inc=1, device_id=(other, sub), device_id_type=MESH)

    loads = [
        pltpu.make_async_copy(start_h, psi0.at[:, 8:264, :], load_sem.at[0]),
        pltpu.make_async_copy(face_h, face_v, load_sem.at[1]),
        pltpu.make_async_copy(slot_h, slot_v, load_sem.at[2]),
        pltpu.make_async_copy(weight_h, weight_s, load_sem.at[3]),
        pltpu.make_async_copy(geom_h, geom, load_sem.at[4]),
    ]
    parts = []
    for n, (low, high) in enumerate(PARTS):
        rows = slice(low, high)
        parts.append([
            pltpu.make_async_copy(far.at[:, rows, :], near.at[:, rows, :], part_sem.at[4 * n + j])
            for j, (far, near) in enumerate(((jac_h, jac), (stab_h, stab), (prec_h, prec), (grad_h, grad)))
        ])
    for load in loads[:4]:
        load.start()
    for part in parts:
        for load in part:
            load.start(priority=1)
    loads[4].start(priority=1)

    zero_plane = jnp.zeros((NV, 8, 128), F32)
    for buf in (psi0, psi1):
        @pl.when(jnp.logical_not(has_left))
        def _():
            buf[:, 0:8, :] = zero_plane

        @pl.when(jnp.logical_not(has_right))
        def _():
            buf[:, 264:272, :] = zero_plane

    loads[0].wait()

    def edge_row(plane):
        return jnp.where(sub == 0, plane[7:8], plane[0:1])

    def pick0(q, carry):
        a = lax.rem(q + 30, 32)
        for v in range(NV):
            nsend0[v, q] = edge_row(psi0[v, pl.ds(pl.multiple_of(8 * a + 8, 8), 8), :])
        return carry

    lax.fori_loop(0, 32, pick0, 0)

    pl.semaphore_wait(barrier, len(peers) + has_other.astype(jnp.int32))

    def a_copies(buf, base):
        right = pltpu.make_async_remote_copy(
            src_ref=buf.at[:, 256:264, :], dst_ref=buf.at[:, 0:8, :],
            send_sem=a_send.at[base], recv_sem=a_recv.at[base],
            device_id=(jnp.minimum(blk + 1, n_blk - 1), sub), device_id_type=MESH)
        left = pltpu.make_async_remote_copy(
            src_ref=buf.at[:, 8:16, :], dst_ref=buf.at[:, 264:272, :],
            send_sem=a_send.at[base + 1], recv_sem=a_recv.at[base + 1],
            device_id=(jnp.maximum(blk - 1, 0), sub), device_id_type=MESH)
        return right, left

    def start_a(buf, base):
        right, left = a_copies(buf, base)

        @pl.when(has_right)
        def _():
            right.start()

        @pl.when(has_left)
        def _():
            left.start()

    def wait_a_recv(buf, base):
        right, left = a_copies(buf, base)

        @pl.when(has_left)
        def _():
            right.wait_recv()

        @pl.when(has_right)
        def _():
            left.wait_recv()

    def wait_a_send(buf, base):
        right, left = a_copies(buf, base)

        @pl.when(has_right)
        def _():
            right.wait_send()

        @pl.when(has_left)
        def _():
            left.wait_send()

    n_copy0 = [
        pltpu.make_async_remote_copy(
            src_ref=nsend0.at[:, low:high], dst_ref=nrecv0.at[:, low:high],
            send_sem=n0_send.at[n], recv_sem=n0_recv.at[n], device_id=partner, device_id_type=MESH)
        for n, (low, high) in enumerate(GHOSTS)]
    n_copy0[0].start()
    start_a(psi0, 0)
    for copy in n_copy0[1:]:
        copy.start()

    around = [near_z + near_x + [partner], near_z, near_z]

    def round_start(n):
        for peer in around[n]:
            pl.semaphore_signal(rounds.at[n], inc=1, device_id=peer, device_id_type=MESH)

    def round_wait(n):
        pl.semaphore_wait(rounds.at[n], len(around[n]))

    round_start(0)

    loads[1].wait()
    loads[2].wait()
    table = slot_v[...]
    for g in range(4):
        patch = face_v[8 * g:8 * g + 8, :]
        lane, high = patch & 127, patch >> 7
        found = jnp.zeros((8, 128), jnp.int32)
        for j in range(16):
            line = jnp.broadcast_to(table[j:j + 1, :], (8, 128))
            found = jnp.where(high == j, jnp.take_along_axis(line, lane, axis=1), found)
        j_, sub_, core_ = found & 7, (found >> 3) & 1, (found >> 4) & 1
        z_, x_, yh_ = (found >> 5) & 7, (found >> 8) & 3, (found >> 10) & 1
        place = jnp.where(yh_ == 0, (x_ << 6) + (z_ << 3), (z_ << 5) + (x_ << 3))
        row = (core_ << 9) + (yh_ << 8) + place + j_
        key[8 * g:8 * g + 8, :] = jnp.where(sub_ == sub, row, -1)

    def fill(q, carry):
        k = jnp.broadcast_to(key[pl.ds(lax.rem(q + 2, 32), 1), :], (16, 128))
        same = (k & 15) == lax.broadcasted_iota(jnp.int32, (16, 128), 0)
        tile = jnp.where(jnp.logical_and(same, k >= 0), k >> 4, -1).astype(F32).astype(BF16)
        one, zero = jnp.ones((16, 128), BF16), jnp.zeros((16, 128), BF16)
        for m in range(64):
            onehot[16 * m:16 * m + 16, pl.ds(pl.multiple_of(q * 128, 128), 128)] = jnp.where(
                tile == jnp.array(m, BF16), one, zero)
        return carry

    def widen(a, carry):
        geom32[a] = geom[pl.ds(pl.multiple_of(a * 256, 256), 256), :].astype(F32)
        return carry

    sub_iota = lax.broadcasted_iota(jnp.int32, (16, 128), 0) & 7
    lane_iota = lax.broadcasted_iota(jnp.int32, (16, 128), 1)
    edge_n = jnp.where(
        sub == 0, jnp.where(sub_iota == 7, -1.0, 0.0), jnp.where(sub_iota == 0, 1.0, 0.0)).astype(F32)

    def sweep_pair(p, buf, halo, halo_row):
        rows = pl.ds(pl.multiple_of(16 * p, 16), 16)
        stab_acc, jac_acc, psi = [None] * NV, [None] * NV, [None] * NV

        def add(total, term):
            return term if total is None else total + term

        for u in range(NV):
            four = buf[u, pl.ds(pl.multiple_of(16 * p, 16), 32), :]
            here = four[8:24]
            psi[u] = here
            d_a = four[0:16] - four[16:32]
            before = jnp.concatenate([pltpu.roll(here[0:8], 1, 0), pltpu.roll(here[8:16], 1, 0)], 0)
            after = jnp.concatenate([pltpu.roll(here[0:8], 7, 0), pltpu.roll(here[8:16], 7, 0)], 0)
            ghost = jnp.concatenate([jnp.broadcast_to(halo[u, halo_row], (8, 128)),
                                     jnp.broadcast_to(halo[u, halo_row + 1], (8, 128))], 0)
            d_n = jnp.where(sub_iota == 0, 0.0, before) - jnp.where(sub_iota == 7, 0.0, after) + edge_n * ghost
            d_c = (jnp.where(lane_iota == 0, 0.0, pltpu.roll(here, 1, 1))
                   - jnp.where(lane_iota == 127, 0.0, pltpu.roll(here, 127, 1)))
            for v in range(NV):
                i = u * NV + v
                stab_acc[v] = add(stab_acc[v], stab[i, rows, :].astype(F32) * here)
                jac_acc[v] = add(jac_acc[v], jac[i, rows, :].astype(F32) * d_a)
                jac_acc[v] = jac_acc[v] + jac[25 + i, rows, :].astype(F32) * d_n
                jac_acc[v] = jac_acc[v] + jac[50 + i, rows, :].astype(F32) * d_c
        resid = [grad[v, rows, :] - stab_acc[v] - 0.5 * jac_acc[v] for v in range(NV)]
        result = []
        for u in range(NV):
            step = None
            for v in range(NV):
                step = add(step, prec[u * NV + v, rows, :].astype(F32) * resid[v])
            result.append(psi[u] + step)
        return result

    def n_copy1(d):
        part = pl.ds(4 * d, 4)
        return pltpu.make_async_remote_copy(
            src_ref=nsend1.at[:, part], dst_ref=nrecv1.at[:, part], send_sem=n_send.at[d], recv_sem=n_recv.at[d],
            device_id=partner, device_id_type=MESH)

    def first_part(s, carry):
        d = jnp.where(s < 2, s + 1, jnp.where(s == 2, 0, s))

        for n, step in enumerate((0, 2, 3, 6)):
            @pl.when(s == step)
            def _():
                for part in PART_OF[n]:
                    for load in parts[part]:
                        load.wait()
                n_copy0[n].wait_recv()
                if n == 1:
                    wait_a_recv(psi0, 0)

        def pair(j, carry):
            p = lax.rem(2 * d + j + 15, 16)
            row = 4 * d + 2 * j
            new = sweep_pair(p, psi0, nrecv0, row)
            for v in range(NV):
                psi1[v, pl.ds(pl.multiple_of(16 * p + 8, 8), 16), :] = new[v]
                nsend1[v, row] = edge_row(new[v][0:8])
                nsend1[v, row + 1] = edge_row(new[v][8:16])
            return carry

        lax.fori_loop(0, 2, pair, 0)
        n_copy1(d).start()

        @pl.when(s == 2)
        def _():
            start_a(psi1, 2)

        return carry

    lax.fori_loop(0, 8, first_part, 0)
    round_wait(0)
    round_start(1)
    lax.fori_loop(0, 32, fill, 0)

    is_wall = core == sub
    not_wall = jnp.logical_not(is_wall)

    def s_copy(k):
        part = pl.ds(pl.multiple_of(8 * k, 8), 8)
        return pltpu.make_async_remote_copy(
            src_ref=sens_loc.at[:, part, :], dst_ref=sens.at[:, part, :], send_sem=s_send.at[k], recv_sem=s_recv.at[k],
            device_id=partner, device_id_type=MESH)

    def wall_row(plane):
        return jnp.where(sub == 0, plane[0:1], plane[7:8])

    loads[3].wait()

    def second_part(s, carry):
        d = lax.rem(s + 1, 8)
        n_copy1(d).wait_recv()

        @pl.when(s == 7)
        def _():
            wait_a_recv(psi1, 2)

        def pair(j, carry):
            p = lax.rem(2 * d + j + 15, 16)
            q = 4 * s + 2 * j
            new = sweep_pair(p, psi1, nrecv1, 4 * d + 2 * j)
            for v in range(NV):
                psi2[v, pl.ds(pl.multiple_of(16 * p, 16), 16), :] = new[v]
            for j in range(2):
                total = weight_s[j, 0] * new[0]
                for v in range(1, NV):
                    total = total + weight_s[j, v] * new[v]
                sens_loc[j, pl.ds(q, 1), :] = wall_row(total[0:8])
                sens_loc[j, pl.ds(q + 1, 1), :] = wall_row(total[8:16])
            return carry

        lax.fori_loop(0, 2, pair, 0)

        @pl.when(jnp.logical_and(is_wall, lax.rem(s, 2) == 1))
        def _():
            k = s // 2
            s_copy(k).start()
            part = pl.ds(pl.multiple_of(8 * k, 8), 8)
            sens[:, part, :] = sens_loc[:, part, :]

        return carry

    lax.fori_loop(0, 8, second_part, 0)
    round_wait(1)
    round_start(2)
    state_copy = pltpu.make_async_copy(psi2, state_h, out_sem)
    state_copy.start()
    loads[4].wait()
    lax.fori_loop(0, 32, widen, 0)

    def make_contrib(k):
        @pl.when(not_wall)
        def _():
            s_copy(k).wait_recv()

        part = pl.ds(pl.multiple_of(8 * k, 8), 8)
        pressure = jnp.transpose(sens[0, part, :])
        shear = jnp.transpose(sens[1, part, :])
        for r in range(8):
            a = lax.rem(8 * k + 2 + r, 32)
            g0 = geom32[a, pl.ds(0, 128, 2), :]
            g1 = geom32[a, pl.ds(1, 128, 2), :]
            c = pressure[:, r:r + 1] * g0 + shear[:, r:r + 1] * g1
            hi = c.astype(BF16)
            lo = (c - hi.astype(F32)).astype(BF16)
            contrib[128 * r:128 * r + 128, 0:128] = hi
            contrib[128 * r:128 * r + 128, 128:256] = lo

    def product(row, rows, k):
        part = onehot[pl.ds(pl.multiple_of(row, 512), rows), pl.ds(pl.multiple_of(k * 1024, 1024), 1024)]
        both = jnp.dot(part, contrib[...], preferred_element_type=F32)
        return both[:, 0:128] + both[:, 128:256]

    acc[...] = jnp.zeros((1024, 128), F32)

    def quarter(k, carry):
        make_contrib(k)
        acc[...] += product(0, 1024, k)
        return carry

    lax.fori_loop(0, 3, quarter, 0)
    make_contrib(3)

    def c_copy(h):
        return pltpu.make_async_remote_copy(
            src_ref=acc.at[pl.ds(pl.multiple_of((1 - core) * 512 + h * 256, 256), 256), :], dst_ref=core_in.at[h],
            send_sem=c_send.at[h], recv_sem=c_recv.at[h], device_id=core_peer, device_id_type=MESH)

    def spread(out, into, send, recv, peer, place, size):
        def copy(d):
            dest = lax.rem(place + d, size)
            rows = out.shape[0] // size
            return pltpu.make_async_remote_copy(
                src_ref=out.at[pl.ds(pl.multiple_of(dest * rows, rows), rows), :], dst_ref=into.at[d - 1],
                send_sem=send.at[d - 1], recv_sem=recv.at[d - 1], device_id=peer[d], device_id_type=MESH)
        return copy

    ax_copy = spread(ax_out, ax_in, ax_send, ax_recv, x_peer, x, NX)
    az_copy = spread(az_out, az_in, az_send, az_recv, z_peer, z, NZ)
    bz_copy = spread(bz_out, bz_in, bz_send, bz_recv, z_peer, z, NZ)
    bx_copy = spread(bx_out, bx_in, bx_send, bx_recv, x_peer, x, NX)
    x_order, z_order = (2, 3, 1), (4, 3, 5, 2, 6, 1, 7)

    def gathered(out, into, copy, place, size):
        rows = out.shape[0] // size
        for d in range(1, size):
            copy(d).wait_recv()
        total = out[pl.ds(pl.multiple_of(place * rows, rows), rows), :]
        for d in range(1, size):
            total = total + into[d - 1]
        return total

    acc[pl.ds(pl.multiple_of((1 - core) * 512, 512), 512), :] += product((1 - core) * 512, 512, 3)
    for h in (1, 0):
        c_copy(h).start()
    acc[pl.ds(pl.multiple_of(core * 512, 512), 512), :] += product(core * 512, 512, 3)

    round_wait(2)
    c_copy(1).wait_recv()
    bz_out[...] = acc[pl.ds(pl.multiple_of(core * 512 + 256, 256), 256), :] + core_in[1]
    for d in z_order:
        bz_copy(d).start()
    c_copy(0).wait_recv()
    ax_out[...] = acc[pl.ds(pl.multiple_of(core * 512, 256), 256), :] + core_in[0]
    for d in x_order:
        ax_copy(d).start()
    az_out[...] = gathered(ax_out, ax_in, ax_copy, x, NX)
    for d in z_order:
        az_copy(d).start()
    bx_out[...] = gathered(bz_out, bz_in, bz_copy, z, NZ)
    for d in x_order:
        bx_copy(d).start()
    y_out[8:16, :] = gathered(bx_out, bx_in, bx_copy, x, NX)
    y_out[0:8, :] = gathered(az_out, az_in, az_copy, z, NZ)

    y_rows = [1 - yh, 1 - yh, yh]

    def y_copy(k):
        return pltpu.make_async_remote_copy(
            src_ref=y_out.at[pl.ds(pl.multiple_of(y_rows[k] * 8, 8), 8), :], dst_ref=y_in.at[k],
            send_sem=y_send.at[k], recv_sem=y_recv.at[k], device_id=y_peer[k], device_id_type=MESH)

    for k in range(3):
        y_copy(k).start()
    for k in range(3):
        y_copy(k).wait_recv()
    mine = pl.ds(pl.multiple_of(8 * sub, 8), 8)
    others = pl.ds(pl.multiple_of(8 * (1 - sub), 8), 8)
    patch_v[mine, :] = y_out[pl.ds(pl.multiple_of(yh * 8, 8), 8), :] + y_in[0]
    patch_v[others, :] = y_in[1] + y_in[2]

    for copy in n_copy0:
        copy.wait_send()
    wait_a_send(psi0, 0)
    wait_a_send(psi1, 2)
    for d in range(8):
        n_copy1(d).wait_send()

    @pl.when(is_wall)
    def _():
        for k in range(4):
            s_copy(k).wait_send()

    for h in range(2):
        c_copy(h).wait_send()
    for d in range(1, NX):
        ax_copy(d).wait_send()
        bx_copy(d).wait_send()
    for d in range(1, NZ):
        az_copy(d).wait_send()
        bz_copy(d).wait_send()
    for k in range(3):
        y_copy(k).wait_send()
    state_copy.wait()


def hand_on(state_in, patch_in, state_out, patch_out, state, patch, in_sem, out_sem):
    pieces = [(patch_in, patch, patch_out)] + [(state_in.at[v], state.at[v], state_out.at[v]) for v in range(NV)]
    enter = [pltpu.make_async_copy(a, b, in_sem.at[n]) for n, (a, b, _) in enumerate(pieces)]
    leave = [pltpu.make_async_copy(b, c, out_sem.at[n]) for n, (_, b, c) in enumerate(pieces)]
    for copy in enter:
        copy.start()
    for n, copy in enumerate(enter):
        copy.wait()
        leave[n].start()
    for copy in leave:
        copy.wait()


def local(
    adjoint_start, objective_grad, flux_jacobian, stab_block, precond_block,
    wall_weight, wall_geometry, face_patch, patch_slot,
):
    any_, vmem = (pl.BlockSpec(memory_space=m) for m in (pl.ANY, pltpu.VMEM))
    dma = pltpu.SemaphoreType.DMA
    state, patch = pl.pallas_call(
        kernel,
        out_shape=(jax.ShapeDtypeStruct((NV, 256, 128), F32), jax.ShapeDtypeStruct((16, 128), F32)),
        in_specs=[any_] * 9,
        out_specs=(any_, vmem),
        scratch_shapes=[
            pltpu.VMEM((NV, 272, 128), F32),
            pltpu.VMEM((NV, 272, 128), F32),
            pltpu.VMEM((NV, 256, 128), F32),
            pltpu.VMEM((NV, 256, 128), F32),
            pltpu.VMEM((75, 256, 128), BF16),
            pltpu.VMEM((25, 256, 128), BF16),
            pltpu.VMEM((25, 256, 128), BF16),
            pltpu.VMEM((8192, 128), BF16),
            pltpu.SMEM((2, NV), F32),
            pltpu.VMEM((32, 128), jnp.int32),
            pltpu.VMEM((16, 128), jnp.int32),
            pltpu.VMEM((32, 256, 128), F32),
            pltpu.VMEM((1024, 4096), BF16),
            pltpu.VMEM((32, 128), jnp.int32),
            pltpu.VMEM((1024, 256), BF16),
            pltpu.VMEM((1024, 128), F32),
            pltpu.VMEM((NV, 32, 1, 128), F32),
            pltpu.VMEM((NV, 32, 1, 128), F32),
            pltpu.VMEM((NV, 32, 1, 128), F32),
            pltpu.VMEM((NV, 32, 1, 128), F32),
            pltpu.VMEM((2, 32, 128), F32),
            pltpu.VMEM((2, 32, 128), F32),
            pltpu.VMEM((2, 256, 128), F32),
            pltpu.VMEM((256, 128), F32),
            pltpu.VMEM((NX - 1, 64, 128), F32),
            pltpu.VMEM((64, 128), F32),
            pltpu.VMEM((NZ - 1, 8, 128), F32),
            pltpu.VMEM((256, 128), F32),
            pltpu.VMEM((NZ - 1, 32, 128), F32),
            pltpu.VMEM((32, 128), F32),
            pltpu.VMEM((NX - 1, 8, 128), F32),
            pltpu.VMEM((16, 128), F32),
            pltpu.VMEM((3, 8, 128), F32),
            pltpu.SemaphoreType.REGULAR((3,)),
            dma((5,)), dma((4 * len(PARTS),)), dma,
            dma((4,)), dma((4,)),
            dma((4,)), dma((4,)), dma((8,)), dma((8,)),
            dma((4,)), dma((4,)),
            dma((2,)), dma((2,)),
            dma((NX - 1,)), dma((NX - 1,)), dma((NZ - 1,)), dma((NZ - 1,)),
            dma((NZ - 1,)), dma((NZ - 1,)), dma((NX - 1,)), dma((NX - 1,)),
            dma((3,)), dma((3,)),
        ],
        compiler_params=pltpu.CompilerParams(
            collective_id=0, has_side_effects=True, vmem_limit_bytes=60 * 1024 * 1024),
    )(
        adjoint_start.reshape(NV, 256, 128),
        objective_grad.reshape(NV, 256, 128),
        flux_jacobian.reshape(75, 256, 128),
        stab_block.reshape(25, 256, 128),
        precond_block.reshape(25, 256, 128),
        wall_weight.T,
        wall_geometry.reshape(8192, 128),
        face_patch.reshape(32, 128),
        patch_slot.reshape(16, 128),
    )
    state, patch = pl.pallas_call(
        hand_on,
        out_shape=(jax.ShapeDtypeStruct(state.shape, F32), jax.ShapeDtypeStruct(patch.shape, F32)),
        in_specs=[any_, any_],
        out_specs=(any_, any_),
        scratch_shapes=[pltpu.VMEM((NV, 256, 128), F32), pltpu.VMEM((16, 128), F32), dma((6,)), dma((6,))],
        compiler_params=pltpu.CompilerParams(vmem_limit_bytes=60 * 1024 * 1024),
    )(state, patch)
    return state.reshape(NV, 32, 8, 128), patch


def solution(mesh):
    return jax.shard_map(
        local,
        mesh=mesh,
        in_specs=(
            P(None, "blk", "sub", None),
            P(None, "blk", "sub", None),
            P(None, None, None, "blk", "sub", None),
            P(None, None, "blk", "sub", None),
            P(None, None, "blk", "sub", None),
            P(),
            P("blk", None, None),
            P("blk"),
            P(),
        ),
        out_specs=(P(None, "blk", "sub", None), P("blk", None)),
        check_vma=False,
    )
```

```python
import functools

import jax
import jax.numpy as jnp
from jax import lax
from jax.experimental import pallas as pl
from jax.experimental.pallas import tpu as pltpu
from jax.sharding import PartitionSpec as P

MESH = pl.DeviceIdType.MESH
F32 = jnp.float32
BF16 = jnp.bfloat16

NV = 5
PARTS = ((16, 80), (0, 16), (240, 256), (80, 176), (176, 240))
PART_OF = ((0,), (1, 2), (3,), (4,))
GHOSTS = ((4, 12), (0, 4), (12, 24), (24, 32))
NX, NZ = 4, 8


def kernel(
    start_h, grad_h, jac_h, stab_h, prec_h, weight_h, geom_h, face_h, slot_h,
    state_h, patch_v,
    psi0, psi1, psi2, grad, jac, stab, prec, geom, weight_s, face_v, slot_v, geom32, onehot, key, contrib, acc,
    nsend0, nrecv0, nsend1, nrecv1, sens_loc, sens,
    core_in, ax_out, ax_in, az_out, az_in, bz_out, bz_in, bx_out, bx_in, y_out, y_in,
    rounds, load_sem, part_sem, out_sem, a_send, a_recv, n0_send, n0_recv, n_send, n_recv, s_send, s_recv,
    c_send, c_recv, ax_send, ax_recv, az_send, az_recv, bz_send, bz_recv, bx_send, bx_recv, y_send, y_recv,
):
    blk, sub = lax.axis_index("blk"), lax.axis_index("sub")
    n_blk = lax.axis_size("blk")
    core = lax.rem(blk, 2)
    z = lax.rem(blk // 2, NZ)
    x = lax.rem(blk // (2 * NZ), NX)
    yh = blk // (2 * NZ * NX)

    def at(yh_, x_, z_, core_):
        return ((yh_ * NX + x_) * NZ + z_) * 2 + core_

    core_peer = (at(yh, x, z, 1 - core), sub)
    x_peer = [(at(yh, lax.rem(x + d, NX), z, core), sub) for d in range(NX)]
    z_peer = [(at(yh, x, lax.rem(z + d, NZ), core), sub) for d in range(NZ)]
    y_peer = [(at(1 - yh, x, z, core), sub), (at(1 - yh, x, z, core), 1 - sub), (blk, 1 - sub)]
    partner = (blk, 1 - sub)
    has_left, has_right = blk > 0, blk < n_blk - 1
    other = jnp.where(core == 1, blk + 1, blk - 1)
    has_other = jnp.logical_and(other >= 0, other < n_blk)

    barrier = pltpu.get_barrier_semaphore()
    near_z, near_x = [z_peer[1], z_peer[NZ - 1]], [x_peer[1], x_peer[NX - 1]]
    peers = [core_peer, y_peer[1], partner] + near_x + near_z
    for peer in peers:
        pl.semaphore_signal(barrier, inc=1, device_id=peer, device_id_type=MESH)

    @pl.when(has_other)
    def _():
        pl.semaphore_signal(barrier, inc=1, device_id=(other, sub), device_id_type=MESH)

    loads = [
        pltpu.make_async_copy(start_h, psi0.at[:, 8:264, :], load_sem.at[0]),
        pltpu.make_async_copy(face_h, face_v, load_sem.at[1]),
        pltpu.make_async_copy(slot_h, slot_v, load_sem.at[2]),
        pltpu.make_async_copy(weight_h, weight_s, load_sem.at[3]),
        pltpu.make_async_copy(geom_h, geom, load_sem.at[4]),
    ]
    parts = []
    for n, (low, high) in enumerate(PARTS):
        rows = slice(low, high)
        parts.append([
            pltpu.make_async_copy(far.at[:, rows, :], near.at[:, rows, :], part_sem.at[4 * n + j])
            for j, (far, near) in enumerate(((jac_h, jac), (stab_h, stab), (prec_h, prec), (grad_h, grad)))
        ])
    for load in loads[:4]:
        load.start()
    for part in parts:
        for load in part:
            load.start(priority=1)
    loads[4].start(priority=1)

    zero_plane = jnp.zeros((NV, 8, 128), F32)
    for buf in (psi0, psi1):
        @pl.when(jnp.logical_not(has_left))
        def _():
            buf[:, 0:8, :] = zero_plane

        @pl.when(jnp.logical_not(has_right))
        def _():
            buf[:, 264:272, :] = zero_plane

    loads[0].wait()

    def edge_row(plane):
        return jnp.where(sub == 0, plane[7:8], plane[0:1])

    def pick0(q, carry):
        a = lax.rem(q + 30, 32)
        for v in range(NV):
            nsend0[v, q] = edge_row(psi0[v, pl.ds(pl.multiple_of(8 * a + 8, 8), 8), :])
        return carry

    lax.fori_loop(0, 32, pick0, 0)

    pl.semaphore_wait(barrier, len(peers) + has_other.astype(jnp.int32))

    def a_copies(buf, base):
        right = pltpu.make_async_remote_copy(
            src_ref=buf.at[:, 256:264, :], dst_ref=buf.at[:, 0:8, :],
            send_sem=a_send.at[base], recv_sem=a_recv.at[base],
            device_id=(jnp.minimum(blk + 1, n_blk - 1), sub), device_id_type=MESH)
        left = pltpu.make_async_remote_copy(
            src_ref=buf.at[:, 8:16, :], dst_ref=buf.at[:, 264:272, :],
            send_sem=a_send.at[base + 1], recv_sem=a_recv.at[base + 1],
            device_id=(jnp.maximum(blk - 1, 0), sub), device_id_type=MESH)
        return right, left

    def start_a(buf, base):
        right, left = a_copies(buf, base)

        @pl.when(has_right)
        def _():
            right.start()

        @pl.when(has_left)
        def _():
            left.start()

    def wait_a_recv(buf, base):
        right, left = a_copies(buf, base)

        @pl.when(has_left)
        def _():
            right.wait_recv()

        @pl.when(has_right)
        def _():
            left.wait_recv()

    def wait_a_send(buf, base):
        right, left = a_copies(buf, base)

        @pl.when(has_right)
        def _():
            right.wait_send()

        @pl.when(has_left)
        def _():
            left.wait_send()

    n_copy0 = [
        pltpu.make_async_remote_copy(
            src_ref=nsend0.at[:, low:high], dst_ref=nrecv0.at[:, low:high],
            send_sem=n0_send.at[n], recv_sem=n0_recv.at[n], device_id=partner, device_id_type=MESH)
        for n, (low, high) in enumerate(GHOSTS)]
    n_copy0[0].start()
    start_a(psi0, 0)
    for copy in n_copy0[1:]:
        copy.start()

    around = [near_z + near_x + [partner], near_z, near_z]

    def round_start(n):
        for peer in around[n]:
            pl.semaphore_signal(rounds.at[n], inc=1, device_id=peer, device_id_type=MESH)

    def round_wait(n):
        pl.semaphore_wait(rounds.at[n], len(around[n]))

    round_start(0)

    loads[1].wait()
    loads[2].wait()
    table = slot_v[...]
    for g in range(4):
        patch = face_v[8 * g:8 * g + 8, :]
        lane, high = patch & 127, patch >> 7
        found = jnp.zeros((8, 128), jnp.int32)
        for j in range(16):
            line = jnp.broadcast_to(table[j:j + 1, :], (8, 128))
            found = jnp.where(high == j, jnp.take_along_axis(line, lane, axis=1), found)
        j_, sub_, core_ = found & 7, (found >> 3) & 1, (found >> 4) & 1
        z_, x_, yh_ = (found >> 5) & 7, (found >> 8) & 3, (found >> 10) & 1
        place = jnp.where(yh_ == 0, (x_ << 6) + (z_ << 3), (z_ << 5) + (x_ << 3))
        row = (core_ << 9) + (yh_ << 8) + place + j_
        key[8 * g:8 * g + 8, :] = jnp.where(sub_ == sub, row, -1)

    def fill(q, carry):
        k = jnp.broadcast_to(key[pl.ds(lax.rem(q + 2, 32), 1), :], (16, 128))
        same = (k & 15) == lax.broadcasted_iota(jnp.int32, (16, 128), 0)
        tile = jnp.where(jnp.logical_and(same, k >= 0), k >> 4, -1).astype(F32).astype(BF16)
        one, zero = jnp.ones((16, 128), BF16), jnp.zeros((16, 128), BF16)
        for m in range(64):
            onehot[16 * m:16 * m + 16, pl.ds(pl.multiple_of(q * 128, 128), 128)] = jnp.where(
                tile == jnp.array(m, BF16), one, zero)
        return carry

    def widen(a, carry):
        geom32[a] = geom[pl.ds(pl.multiple_of(a * 256, 256), 256), :].astype(F32)
        return carry

    sub_iota = lax.broadcasted_iota(jnp.int32, (16, 128), 0) & 7
    lane_iota = lax.broadcasted_iota(jnp.int32, (16, 128), 1)
    edge_n = jnp.where(
        sub == 0, jnp.where(sub_iota == 7, -1.0, 0.0), jnp.where(sub_iota == 0, 1.0, 0.0)).astype(F32)

    def sweep_pair(p, buf, halo, halo_row):
        rows = pl.ds(pl.multiple_of(16 * p, 16), 16)
        stab_acc, jac_acc, psi = [None] * NV, [None] * NV, [None] * NV

        def add(total, term):
            return term if total is None else total + term

        for u in range(NV):
            four = buf[u, pl.ds(pl.multiple_of(16 * p, 16), 32), :]
            here = four[8:24]
            psi[u] = here
            d_a = four[0:16] - four[16:32]
            before = jnp.concatenate([pltpu.roll(here[0:8], 1, 0), pltpu.roll(here[8:16], 1, 0)], 0)
            after = jnp.concatenate([pltpu.roll(here[0:8], 7, 0), pltpu.roll(here[8:16], 7, 0)], 0)
            ghost = jnp.concatenate([jnp.broadcast_to(halo[u, halo_row], (8, 128)),
                                     jnp.broadcast_to(halo[u, halo_row + 1], (8, 128))], 0)
            d_n = jnp.where(sub_iota == 0, 0.0, before) - jnp.where(sub_iota == 7, 0.0, after) + edge_n * ghost
            d_c = (jnp.where(lane_iota == 0, 0.0, pltpu.roll(here, 1, 1))
                   - jnp.where(lane_iota == 127, 0.0, pltpu.roll(here, 127, 1)))
            for v in range(NV):
                i = u * NV + v
                stab_acc[v] = add(stab_acc[v], stab[i, rows, :].astype(F32) * here)
                jac_acc[v] = add(jac_acc[v], jac[i, rows, :].astype(F32) * d_a)
                jac_acc[v] = jac_acc[v] + jac[25 + i, rows, :].astype(F32) * d_n
                jac_acc[v] = jac_acc[v] + jac[50 + i, rows, :].astype(F32) * d_c
        resid = [grad[v, rows, :] - stab_acc[v] - 0.5 * jac_acc[v] for v in range(NV)]
        result = []
        for u in range(NV):
            step = None
            for v in range(NV):
                step = add(step, prec[u * NV + v, rows, :].astype(F32) * resid[v])
            result.append(psi[u] + step)
        return result

    lax.fori_loop(0, 32, fill, 0)

    def n_copy1(d):
        part = pl.ds(4 * d, 4)
        return pltpu.make_async_remote_copy(
            src_ref=nsend1.at[:, part], dst_ref=nrecv1.at[:, part], send_sem=n_send.at[d], recv_sem=n_recv.at[d],
            device_id=partner, device_id_type=MESH)

    def first_part(s, carry):
        d = jnp.where(s < 2, s + 1, jnp.where(s == 2, 0, s))

        for n, step in enumerate((0, 2, 3, 6)):
            @pl.when(s == step)
            def _():
                for part in PART_OF[n]:
                    for load in parts[part]:
                        load.wait()
                n_copy0[n].wait_recv()
                if n == 1:
                    wait_a_recv(psi0, 0)

        def pair(j, carry):
            p = lax.rem(2 * d + j + 15, 16)
            row = 4 * d + 2 * j
            new = sweep_pair(p, psi0, nrecv0, row)
            for v in range(NV):
                psi1[v, pl.ds(pl.multiple_of(16 * p + 8, 8), 16), :] = new[v]
                nsend1[v, row] = edge_row(new[v][0:8])
                nsend1[v, row + 1] = edge_row(new[v][8:16])
            return carry

        lax.fori_loop(0, 2, pair, 0)
        n_copy1(d).start()

        @pl.when(s == 2)
        def _():
            start_a(psi1, 2)

        return carry

    lax.fori_loop(0, 8, first_part, 0)
    round_wait(0)
    round_start(1)
    loads[4].wait()
    lax.fori_loop(0, 32, widen, 0)

    is_wall = core == sub
    not_wall = jnp.logical_not(is_wall)

    def s_copy(k):
        part = pl.ds(pl.multiple_of(8 * k, 8), 8)
        return pltpu.make_async_remote_copy(
            src_ref=sens_loc.at[:, part, :], dst_ref=sens.at[:, part, :], send_sem=s_send.at[k], recv_sem=s_recv.at[k],
            device_id=partner, device_id_type=MESH)

    def wall_row(plane):
        return jnp.where(sub == 0, plane[0:1], plane[7:8])

    loads[3].wait()

    def second_part(s, carry):
        d = lax.rem(s + 1, 8)
        n_copy1(d).wait_recv()

        @pl.when(s == 7)
        def _():
            wait_a_recv(psi1, 2)

        def pair(j, carry):
            p = lax.rem(2 * d + j + 15, 16)
            q = 4 * s + 2 * j
            new = sweep_pair(p, psi1, nrecv1, 4 * d + 2 * j)
            for v in range(NV):
                psi2[v, pl.ds(pl.multiple_of(16 * p, 16), 16), :] = new[v]
            for j in range(2):
                total = weight_s[j, 0] * new[0]
                for v in range(1, NV):
                    total = total + weight_s[j, v] * new[v]
                sens_loc[j, pl.ds(q, 1), :] = wall_row(total[0:8])
                sens_loc[j, pl.ds(q + 1, 1), :] = wall_row(total[8:16])
            return carry

        lax.fori_loop(0, 2, pair, 0)

        @pl.when(jnp.logical_and(is_wall, lax.rem(s, 2) == 1))
        def _():
            k = s // 2
            s_copy(k).start()
            part = pl.ds(pl.multiple_of(8 * k, 8), 8)
            sens[:, part, :] = sens_loc[:, part, :]

        return carry

    lax.fori_loop(0, 8, second_part, 0)
    round_wait(1)
    round_start(2)
    state_copy = pltpu.make_async_copy(psi2, state_h, out_sem)
    state_copy.start()

    def make_contrib(k):
        @pl.when(not_wall)
        def _():
            s_copy(k).wait_recv()

        part = pl.ds(pl.multiple_of(8 * k, 8), 8)
        pressure = jnp.transpose(sens[0, part, :])
        shear = jnp.transpose(sens[1, part, :])
        for r in range(8):
            a = lax.rem(8 * k + 2 + r, 32)
            g0 = geom32[a, pl.ds(0, 128, 2), :]
            g1 = geom32[a, pl.ds(1, 128, 2), :]
            c = pressure[:, r:r + 1] * g0 + shear[:, r:r + 1] * g1
            hi = c.astype(BF16)
            lo = (c - hi.astype(F32)).astype(BF16)
            contrib[128 * r:128 * r + 128, 0:128] = hi
            contrib[128 * r:128 * r + 128, 128:256] = lo

    def product(row, rows, k):
        part = onehot[pl.ds(pl.multiple_of(row, 512), rows), pl.ds(pl.multiple_of(k * 1024, 1024), 1024)]
        both = jnp.dot(part, contrib[...], preferred_element_type=F32)
        return both[:, 0:128] + both[:, 128:256]

    acc[...] = jnp.zeros((1024, 128), F32)

    def quarter(k, carry):
        make_contrib(k)
        acc[...] += product(0, 1024, k)
        return carry

    lax.fori_loop(0, 3, quarter, 0)
    make_contrib(3)

    def c_copy(h):
        return pltpu.make_async_remote_copy(
            src_ref=acc.at[pl.ds(pl.multiple_of((1 - core) * 512 + h * 256, 256), 256), :], dst_ref=core_in.at[h],
            send_sem=c_send.at[h], recv_sem=c_recv.at[h], device_id=core_peer, device_id_type=MESH)

    def spread(out, into, send, recv, peer, place, size):
        def copy(d):
            dest = lax.rem(place + d, size)
            rows = out.shape[0] // size
            return pltpu.make_async_remote_copy(
                src_ref=out.at[pl.ds(pl.multiple_of(dest * rows, rows), rows), :], dst_ref=into.at[d - 1],
                send_sem=send.at[d - 1], recv_sem=recv.at[d - 1], device_id=peer[d], device_id_type=MESH)
        return copy

    ax_copy = spread(ax_out, ax_in, ax_send, ax_recv, x_peer, x, NX)
    az_copy = spread(az_out, az_in, az_send, az_recv, z_peer, z, NZ)
    bz_copy = spread(bz_out, bz_in, bz_send, bz_recv, z_peer, z, NZ)
    bx_copy = spread(bx_out, bx_in, bx_send, bx_recv, x_peer, x, NX)
    x_order, z_order = (2, 3, 1), (4, 3, 5, 2, 6, 1, 7)

    def gathered(out, into, copy, place, size):
        rows = out.shape[0] // size
        for d in range(1, size):
            copy(d).wait_recv()
        total = out[pl.ds(pl.multiple_of(place * rows, rows), rows), :]
        for d in range(1, size):
            total = total + into[d - 1]
        return total

    acc[pl.ds(pl.multiple_of((1 - core) * 512, 512), 512), :] += product((1 - core) * 512, 512, 3)
    for h in (1, 0):
        c_copy(h).start()
    acc[pl.ds(pl.multiple_of(core * 512, 512), 512), :] += product(core * 512, 512, 3)

    round_wait(2)
    c_copy(1).wait_recv()
    bz_out[...] = acc[pl.ds(pl.multiple_of(core * 512 + 256, 256), 256), :] + core_in[1]
    for d in z_order:
        bz_copy(d).start()
    c_copy(0).wait_recv()
    ax_out[...] = acc[pl.ds(pl.multiple_of(core * 512, 256), 256), :] + core_in[0]
    for d in x_order:
        ax_copy(d).start()
    az_out[...] = gathered(ax_out, ax_in, ax_copy, x, NX)
    for d in z_order:
        az_copy(d).start()
    bx_out[...] = gathered(bz_out, bz_in, bz_copy, z, NZ)
    for d in x_order:
        bx_copy(d).start()
    y_out[8:16, :] = gathered(bx_out, bx_in, bx_copy, x, NX)
    y_out[0:8, :] = gathered(az_out, az_in, az_copy, z, NZ)

    y_rows = [1 - yh, 1 - yh, yh]

    def y_copy(k):
        return pltpu.make_async_remote_copy(
            src_ref=y_out.at[pl.ds(pl.multiple_of(y_rows[k] * 8, 8), 8), :], dst_ref=y_in.at[k],
            send_sem=y_send.at[k], recv_sem=y_recv.at[k], device_id=y_peer[k], device_id_type=MESH)

    for k in range(3):
        y_copy(k).start()
    for k in range(3):
        y_copy(k).wait_recv()
    mine = pl.ds(pl.multiple_of(8 * sub, 8), 8)
    others = pl.ds(pl.multiple_of(8 * (1 - sub), 8), 8)
    patch_v[mine, :] = y_out[pl.ds(pl.multiple_of(yh * 8, 8), 8), :] + y_in[0]
    patch_v[others, :] = y_in[1] + y_in[2]

    for copy in n_copy0:
        copy.wait_send()
    wait_a_send(psi0, 0)
    wait_a_send(psi1, 2)
    for d in range(8):
        n_copy1(d).wait_send()

    @pl.when(is_wall)
    def _():
        for k in range(4):
            s_copy(k).wait_send()

    for h in range(2):
        c_copy(h).wait_send()
    for d in range(1, NX):
        ax_copy(d).wait_send()
        bx_copy(d).wait_send()
    for d in range(1, NZ):
        az_copy(d).wait_send()
        bz_copy(d).wait_send()
    for k in range(3):
        y_copy(k).wait_send()
    state_copy.wait()


def hand_on(state_in, patch_in, state_out, patch_out, state, patch, in_sem, out_sem):
    pieces = [(patch_in, patch, patch_out)] + [(state_in.at[v], state.at[v], state_out.at[v]) for v in range(NV)]
    enter = [pltpu.make_async_copy(a, b, in_sem.at[n]) for n, (a, b, _) in enumerate(pieces)]
    leave = [pltpu.make_async_copy(b, c, out_sem.at[n]) for n, (_, b, c) in enumerate(pieces)]
    for copy in enter:
        copy.start()
    for n, copy in enumerate(enter):
        copy.wait()
        leave[n].start()
    for copy in leave:
        copy.wait()


def local(
    adjoint_start, objective_grad, flux_jacobian, stab_block, precond_block,
    wall_weight, wall_geometry, face_patch, patch_slot,
):
    any_, vmem = (pl.BlockSpec(memory_space=m) for m in (pl.ANY, pltpu.VMEM))
    dma = pltpu.SemaphoreType.DMA
    state, patch = pl.pallas_call(
        kernel,
        out_shape=(jax.ShapeDtypeStruct((NV, 256, 128), F32), jax.ShapeDtypeStruct((16, 128), F32)),
        in_specs=[any_] * 9,
        out_specs=(any_, vmem),
        scratch_shapes=[
            pltpu.VMEM((NV, 272, 128), F32),
            pltpu.VMEM((NV, 272, 128), F32),
            pltpu.VMEM((NV, 256, 128), F32),
            pltpu.VMEM((NV, 256, 128), F32),
            pltpu.VMEM((75, 256, 128), BF16),
            pltpu.VMEM((25, 256, 128), BF16),
            pltpu.VMEM((25, 256, 128), BF16),
            pltpu.VMEM((8192, 128), BF16),
            pltpu.SMEM((2, NV), F32),
            pltpu.VMEM((32, 128), jnp.int32),
            pltpu.VMEM((16, 128), jnp.int32),
            pltpu.VMEM((32, 256, 128), F32),
            pltpu.VMEM((1024, 4096), BF16),
            pltpu.VMEM((32, 128), jnp.int32),
            pltpu.VMEM((1024, 256), BF16),
            pltpu.VMEM((1024, 128), F32),
            pltpu.VMEM((NV, 32, 1, 128), F32),
            pltpu.VMEM((NV, 32, 1, 128), F32),
            pltpu.VMEM((NV, 32, 1, 128), F32),
            pltpu.VMEM((NV, 32, 1, 128), F32),
            pltpu.VMEM((2, 32, 128), F32),
            pltpu.VMEM((2, 32, 128), F32),
            pltpu.VMEM((2, 256, 128), F32),
            pltpu.VMEM((256, 128), F32),
            pltpu.VMEM((NX - 1, 64, 128), F32),
            pltpu.VMEM((64, 128), F32),
            pltpu.VMEM((NZ - 1, 8, 128), F32),
            pltpu.VMEM((256, 128), F32),
            pltpu.VMEM((NZ - 1, 32, 128), F32),
            pltpu.VMEM((32, 128), F32),
            pltpu.VMEM((NX - 1, 8, 128), F32),
            pltpu.VMEM((16, 128), F32),
            pltpu.VMEM((3, 8, 128), F32),
            pltpu.SemaphoreType.REGULAR((3,)),
            dma((5,)), dma((4 * len(PARTS),)), dma,
            dma((4,)), dma((4,)),
            dma((4,)), dma((4,)), dma((8,)), dma((8,)),
            dma((4,)), dma((4,)),
            dma((2,)), dma((2,)),
            dma((NX - 1,)), dma((NX - 1,)), dma((NZ - 1,)), dma((NZ - 1,)),
            dma((NZ - 1,)), dma((NZ - 1,)), dma((NX - 1,)), dma((NX - 1,)),
            dma((3,)), dma((3,)),
        ],
        compiler_params=pltpu.CompilerParams(
            collective_id=0, has_side_effects=True, vmem_limit_bytes=60 * 1024 * 1024),
    )(
        adjoint_start.reshape(NV, 256, 128),
        objective_grad.reshape(NV, 256, 128),
        flux_jacobian.reshape(75, 256, 128),
        stab_block.reshape(25, 256, 128),
        precond_block.reshape(25, 256, 128),
        wall_weight.T,
        wall_geometry.reshape(8192, 128),
        face_patch.reshape(32, 128),
        patch_slot.reshape(16, 128),
    )
    state, patch = pl.pallas_call(
        hand_on,
        out_shape=(jax.ShapeDtypeStruct(state.shape, F32), jax.ShapeDtypeStruct(patch.shape, F32)),
        in_specs=[any_, any_],
        out_specs=(any_, any_),
        scratch_shapes=[pltpu.VMEM((NV, 256, 128), F32), pltpu.VMEM((16, 128), F32), dma((6,)), dma((6,))],
        compiler_params=pltpu.CompilerParams(vmem_limit_bytes=60 * 1024 * 1024),
    )(state, patch)
    return state.reshape(NV, 32, 8, 128), patch


def solution(mesh):
    return jax.shard_map(
        local,
        mesh=mesh,
        in_specs=(
            P(None, "blk", "sub", None),
            P(None, "blk", "sub", None),
            P(None, None, None, "blk", "sub", None),
            P(None, None, "blk", "sub", None),
            P(None, None, "blk", "sub", None),
            P(),
            P("blk", None, None),
            P("blk"),
            P(),
        ),
        out_specs=(P(None, "blk", "sub", None), P("blk", None)),
        check_vma=False,
    )
```

```python
import functools

import jax
import jax.numpy as jnp
from jax import lax
from jax.experimental import pallas as pl
from jax.experimental.pallas import tpu as pltpu
from jax.sharding import PartitionSpec as P

MESH = pl.DeviceIdType.MESH
F32 = jnp.float32
BF16 = jnp.bfloat16

NV = 5
PARTS = ((16, 80), (0, 16), (240, 256), (80, 176), (176, 240))
PART_OF = ((0,), (1, 2), (3,), (4,))
GHOSTS = ((4, 12), (0, 4), (12, 24), (24, 32))
NX, NZ = 4, 8


def kernel(
    start_h, grad_h, jac_h, stab_h, prec_h, weight_h, geom_h, face_h, slot_h,
    state_h, patch_v,
    psi0, psi1, psi2, grad, jac, stab, prec, geom, weight_s, face_v, slot_v, geom32, onehot, key, contrib_a, contrib_b, acc,
    nsend0, nrecv0, nsend1, nrecv1, sens_loc, sens,
    core_in, ax_out, ax_in, az_out, az_in, bz_out, bz_in, bx_out, bx_in, y_out, y_in,
    rounds, load_sem, part_sem, out_sem, a_send, a_recv, n0_send, n0_recv, n_send, n_recv, s_send, s_recv,
    c_send, c_recv, ax_send, ax_recv, az_send, az_recv, bz_send, bz_recv, bx_send, bx_recv, y_send, y_recv,
):
    blk, sub = lax.axis_index("blk"), lax.axis_index("sub")
    n_blk = lax.axis_size("blk")
    core = lax.rem(blk, 2)
    z = lax.rem(blk // 2, NZ)
    x = lax.rem(blk // (2 * NZ), NX)
    yh = blk // (2 * NZ * NX)

    def at(yh_, x_, z_, core_):
        return ((yh_ * NX + x_) * NZ + z_) * 2 + core_

    core_peer = (at(yh, x, z, 1 - core), sub)
    x_peer = [(at(yh, lax.rem(x + d, NX), z, core), sub) for d in range(NX)]
    z_peer = [(at(yh, x, lax.rem(z + d, NZ), core), sub) for d in range(NZ)]
    y_peer = [(at(1 - yh, x, z, core), sub), (at(1 - yh, x, z, core), 1 - sub), (blk, 1 - sub)]
    partner = (blk, 1 - sub)
    has_left, has_right = blk > 0, blk < n_blk - 1
    other = jnp.where(core == 1, blk + 1, blk - 1)
    has_other = jnp.logical_and(other >= 0, other < n_blk)

    barrier = pltpu.get_barrier_semaphore()
    near_z, near_x = [z_peer[1], z_peer[NZ - 1]], [x_peer[1], x_peer[NX - 1]]
    peers = [core_peer, y_peer[1], partner] + near_x + near_z
    for peer in peers:
        pl.semaphore_signal(barrier, inc=1, device_id=peer, device_id_type=MESH)

    @pl.when(has_other)
    def _():
        pl.semaphore_signal(barrier, inc=1, device_id=(other, sub), device_id_type=MESH)

    loads = [
        pltpu.make_async_copy(start_h, psi0.at[:, 8:264, :], load_sem.at[0]),
        pltpu.make_async_copy(face_h, face_v, load_sem.at[1]),
        pltpu.make_async_copy(slot_h, slot_v, load_sem.at[2]),
        pltpu.make_async_copy(weight_h, weight_s, load_sem.at[3]),
        pltpu.make_async_copy(geom_h, geom, load_sem.at[4]),
    ]
    parts = []
    for n, (low, high) in enumerate(PARTS):
        rows = slice(low, high)
        parts.append([
            pltpu.make_async_copy(far.at[:, rows, :], near.at[:, rows, :], part_sem.at[4 * n + j])
            for j, (far, near) in enumerate(((jac_h, jac), (stab_h, stab), (prec_h, prec), (grad_h, grad)))
        ])
    for load in loads[:4]:
        load.start()
    for part in parts:
        for load in part:
            load.start(priority=1)
    loads[4].start(priority=1)

    zero_plane = jnp.zeros((NV, 8, 128), F32)
    for buf in (psi0, psi1):
        @pl.when(jnp.logical_not(has_left))
        def _():
            buf[:, 0:8, :] = zero_plane

        @pl.when(jnp.logical_not(has_right))
        def _():
            buf[:, 264:272, :] = zero_plane

    loads[0].wait()

    def edge_row(plane):
        return jnp.where(sub == 0, plane[7:8], plane[0:1])

    def pick0(q, carry):
        a = lax.rem(q + 30, 32)
        for v in range(NV):
            nsend0[v, q] = edge_row(psi0[v, pl.ds(pl.multiple_of(8 * a + 8, 8), 8), :])
        return carry

    lax.fori_loop(0, 32, pick0, 0)

    pl.semaphore_wait(barrier, len(peers) + has_other.astype(jnp.int32))

    def a_copies(buf, base):
        right = pltpu.make_async_remote_copy(
            src_ref=buf.at[:, 256:264, :], dst_ref=buf.at[:, 0:8, :],
            send_sem=a_send.at[base], recv_sem=a_recv.at[base],
            device_id=(jnp.minimum(blk + 1, n_blk - 1), sub), device_id_type=MESH)
        left = pltpu.make_async_remote_copy(
            src_ref=buf.at[:, 8:16, :], dst_ref=buf.at[:, 264:272, :],
            send_sem=a_send.at[base + 1], recv_sem=a_recv.at[base + 1],
            device_id=(jnp.maximum(blk - 1, 0), sub), device_id_type=MESH)
        return right, left

    def start_a(buf, base):
        right, left = a_copies(buf, base)

        @pl.when(has_right)
        def _():
            right.start()

        @pl.when(has_left)
        def _():
            left.start()

    def wait_a_recv(buf, base):
        right, left = a_copies(buf, base)

        @pl.when(has_left)
        def _():
            right.wait_recv()

        @pl.when(has_right)
        def _():
            left.wait_recv()

    def wait_a_send(buf, base):
        right, left = a_copies(buf, base)

        @pl.when(has_right)
        def _():
            right.wait_send()

        @pl.when(has_left)
        def _():
            left.wait_send()

    n_copy0 = [
        pltpu.make_async_remote_copy(
            src_ref=nsend0.at[:, low:high], dst_ref=nrecv0.at[:, low:high],
            send_sem=n0_send.at[n], recv_sem=n0_recv.at[n], device_id=partner, device_id_type=MESH)
        for n, (low, high) in enumerate(GHOSTS)]
    n_copy0[0].start()
    start_a(psi0, 0)
    for copy in n_copy0[1:]:
        copy.start()

    around = [near_z + near_x + [partner], near_z, near_z]

    def round_start(n):
        for peer in around[n]:
            pl.semaphore_signal(rounds.at[n], inc=1, device_id=peer, device_id_type=MESH)

    def round_wait(n):
        pl.semaphore_wait(rounds.at[n], len(around[n]))

    round_start(0)

    loads[1].wait()
    loads[2].wait()
    table = slot_v[...]
    for g in range(4):
        patch = face_v[8 * g:8 * g + 8, :]
        lane, high = patch & 127, patch >> 7
        found = jnp.zeros((8, 128), jnp.int32)
        for j in range(16):
            line = jnp.broadcast_to(table[j:j + 1, :], (8, 128))
            found = jnp.where(high == j, jnp.take_along_axis(line, lane, axis=1), found)
        j_, sub_, core_ = found & 7, (found >> 3) & 1, (found >> 4) & 1
        z_, x_, yh_ = (found >> 5) & 7, (found >> 8) & 3, (found >> 10) & 1
        place = jnp.where(yh_ == 0, (x_ << 6) + (z_ << 3), (z_ << 5) + (x_ << 3))
        row = (core_ << 9) + (yh_ << 8) + place + j_
        key[8 * g:8 * g + 8, :] = jnp.where(sub_ == sub, row, -1)

    def fill(q, carry):
        k = jnp.broadcast_to(key[pl.ds(lax.rem(q + 2, 32), 1), :], (16, 128))
        same = (k & 15) == lax.broadcasted_iota(jnp.int32, (16, 128), 0)
        tile = jnp.where(jnp.logical_and(same, k >= 0), k >> 4, -1).astype(F32).astype(BF16)
        one, zero = jnp.ones((16, 128), BF16), jnp.zeros((16, 128), BF16)
        for m in range(64):
            onehot[16 * m:16 * m + 16, pl.ds(pl.multiple_of(q * 128, 128), 128)] = jnp.where(
                tile == jnp.array(m, BF16), one, zero)
        return carry

    def widen(a, carry):
        geom32[a] = geom[pl.ds(pl.multiple_of(a * 256, 256), 256), :].astype(F32)
        return carry

    sub_iota = lax.broadcasted_iota(jnp.int32, (16, 128), 0) & 7
    lane_iota = lax.broadcasted_iota(jnp.int32, (16, 128), 1)
    edge_n = jnp.where(
        sub == 0, jnp.where(sub_iota == 7, -1.0, 0.0), jnp.where(sub_iota == 0, 1.0, 0.0)).astype(F32)

    def sweep_pair(p, buf, halo, halo_row):
        rows = pl.ds(pl.multiple_of(16 * p, 16), 16)
        stab_acc, jac_acc, psi = [None] * NV, [None] * NV, [None] * NV

        def add(total, term):
            return term if total is None else total + term

        for u in range(NV):
            four = buf[u, pl.ds(pl.multiple_of(16 * p, 16), 32), :]
            here = four[8:24]
            psi[u] = here
            d_a = four[0:16] - four[16:32]
            before = jnp.concatenate([pltpu.roll(here[0:8], 1, 0), pltpu.roll(here[8:16], 1, 0)], 0)
            after = jnp.concatenate([pltpu.roll(here[0:8], 7, 0), pltpu.roll(here[8:16], 7, 0)], 0)
            ghost = jnp.concatenate([jnp.broadcast_to(halo[u, halo_row], (8, 128)),
                                     jnp.broadcast_to(halo[u, halo_row + 1], (8, 128))], 0)
            d_n = jnp.where(sub_iota == 0, 0.0, before) - jnp.where(sub_iota == 7, 0.0, after) + edge_n * ghost
            d_c = (jnp.where(lane_iota == 0, 0.0, pltpu.roll(here, 1, 1))
                   - jnp.where(lane_iota == 127, 0.0, pltpu.roll(here, 127, 1)))
            for v in range(NV):
                i = u * NV + v
                stab_acc[v] = add(stab_acc[v], stab[i, rows, :].astype(F32) * here)
                jac_acc[v] = add(jac_acc[v], jac[i, rows, :].astype(F32) * d_a)
                jac_acc[v] = jac_acc[v] + jac[25 + i, rows, :].astype(F32) * d_n
                jac_acc[v] = jac_acc[v] + jac[50 + i, rows, :].astype(F32) * d_c
        resid = [grad[v, rows, :] - stab_acc[v] - 0.5 * jac_acc[v] for v in range(NV)]
        result = []
        for u in range(NV):
            step = None
            for v in range(NV):
                step = add(step, prec[u * NV + v, rows, :].astype(F32) * resid[v])
            result.append(psi[u] + step)
        return result

    lax.fori_loop(0, 32, fill, 0)

    def n_copy1(d):
        part = pl.ds(4 * d, 4)
        return pltpu.make_async_remote_copy(
            src_ref=nsend1.at[:, part], dst_ref=nrecv1.at[:, part], send_sem=n_send.at[d], recv_sem=n_recv.at[d],
            device_id=partner, device_id_type=MESH)

    def first_part(s, carry):
        d = jnp.where(s < 2, s + 1, jnp.where(s == 2, 0, s))

        for n, step in enumerate((0, 2, 3, 6)):
            @pl.when(s == step)
            def _():
                for part in PART_OF[n]:
                    for load in parts[part]:
                        load.wait()
                n_copy0[n].wait_recv()
                if n == 1:
                    wait_a_recv(psi0, 0)

        def pair(j, carry):
            p = lax.rem(2 * d + j + 15, 16)
            row = 4 * d + 2 * j
            new = sweep_pair(p, psi0, nrecv0, row)
            for v in range(NV):
                psi1[v, pl.ds(pl.multiple_of(16 * p + 8, 8), 16), :] = new[v]
                nsend1[v, row] = edge_row(new[v][0:8])
                nsend1[v, row + 1] = edge_row(new[v][8:16])
            return carry

        lax.fori_loop(0, 2, pair, 0)
        n_copy1(d).start()

        @pl.when(s == 2)
        def _():
            start_a(psi1, 2)

        return carry

    lax.fori_loop(0, 8, first_part, 0)
    round_wait(0)
    round_start(1)
    loads[4].wait()
    lax.fori_loop(0, 32, widen, 0)

    is_wall = core == sub
    not_wall = jnp.logical_not(is_wall)

    def s_copy(k):
        part = pl.ds(pl.multiple_of(8 * k, 8), 8)
        return pltpu.make_async_remote_copy(
            src_ref=sens_loc.at[:, part, :], dst_ref=sens.at[:, part, :], send_sem=s_send.at[k], recv_sem=s_recv.at[k],
            device_id=partner, device_id_type=MESH)

    def wall_row(plane):
        return jnp.where(sub == 0, plane[0:1], plane[7:8])

    loads[3].wait()

    def second_part(s, carry):
        d = lax.rem(s + 1, 8)
        n_copy1(d).wait_recv()

        @pl.when(s == 7)
        def _():
            wait_a_recv(psi1, 2)

        def pair(j, carry):
            p = lax.rem(2 * d + j + 15, 16)
            q = 4 * s + 2 * j
            new = sweep_pair(p, psi1, nrecv1, 4 * d + 2 * j)
            for v in range(NV):
                psi2[v, pl.ds(pl.multiple_of(16 * p, 16), 16), :] = new[v]
            for j in range(2):
                total = weight_s[j, 0] * new[0]
                for v in range(1, NV):
                    total = total + weight_s[j, v] * new[v]
                sens_loc[j, pl.ds(q, 1), :] = wall_row(total[0:8])
                sens_loc[j, pl.ds(q + 1, 1), :] = wall_row(total[8:16])
            return carry

        lax.fori_loop(0, 2, pair, 0)

        @pl.when(jnp.logical_and(is_wall, lax.rem(s, 2) == 1))
        def _():
            k = s // 2
            s_copy(k).start()
            part = pl.ds(pl.multiple_of(8 * k, 8), 8)
            sens[:, part, :] = sens_loc[:, part, :]

        return carry

    lax.fori_loop(0, 8, second_part, 0)
    round_wait(1)
    round_start(2)
    state_copy = pltpu.make_async_copy(psi2, state_h, out_sem)
    state_copy.start()

    def make_contrib(k):
        contrib = (contrib_a, contrib_b)[k % 2]

        @pl.when(not_wall)
        def _():
            s_copy(k).wait_recv()

        part = pl.ds(pl.multiple_of(8 * k, 8), 8)
        pressure = jnp.transpose(sens[0, part, :])
        shear = jnp.transpose(sens[1, part, :])
        for r in range(8):
            a = (8 * k + 2 + r) % 32
            g0 = geom32[a, pl.ds(0, 128, 2), :]
            g1 = geom32[a, pl.ds(1, 128, 2), :]
            c = pressure[:, r:r + 1] * g0 + shear[:, r:r + 1] * g1
            hi = c.astype(BF16)
            lo = (c - hi.astype(F32)).astype(BF16)
            contrib[128 * r:128 * r + 128, 0:128] = hi
            contrib[128 * r:128 * r + 128, 128:256] = lo

    def product(row, rows, k):
        part = onehot[pl.ds(pl.multiple_of(row, 512), rows), pl.ds(pl.multiple_of(k * 1024, 1024), 1024)]
        contrib = (contrib_a, contrib_b)[k % 2]
        both = jnp.dot(part, contrib[...], preferred_element_type=F32)
        return both[:, 0:128] + both[:, 128:256]

    make_contrib(0)
    for k in range(3):
        make_contrib(k + 1)
        total = product(0, 1024, k)
        acc[...] = total if k == 0 else acc[...] + total

    def c_copy(h):
        return pltpu.make_async_remote_copy(
            src_ref=acc.at[pl.ds(pl.multiple_of((1 - core) * 512 + h * 256, 256), 256), :], dst_ref=core_in.at[h],
            send_sem=c_send.at[h], recv_sem=c_recv.at[h], device_id=core_peer, device_id_type=MESH)

    def spread(out, into, send, recv, peer, place, size):
        def copy(d):
            dest = lax.rem(place + d, size)
            rows = out.shape[0] // size
            return pltpu.make_async_remote_copy(
                src_ref=out.at[pl.ds(pl.multiple_of(dest * rows, rows), rows), :], dst_ref=into.at[d - 1],
                send_sem=send.at[d - 1], recv_sem=recv.at[d - 1], device_id=peer[d], device_id_type=MESH)
        return copy

    ax_copy = spread(ax_out, ax_in, ax_send, ax_recv, x_peer, x, NX)
    az_copy = spread(az_out, az_in, az_send, az_recv, z_peer, z, NZ)
    bz_copy = spread(bz_out, bz_in, bz_send, bz_recv, z_peer, z, NZ)
    bx_copy = spread(bx_out, bx_in, bx_send, bx_recv, x_peer, x, NX)
    x_order, z_order = (2, 3, 1), (4, 3, 5, 2, 6, 1, 7)

    def gathered(out, into, copy, place, size):
        rows = out.shape[0] // size
        for d in range(1, size):
            copy(d).wait_recv()
        total = out[pl.ds(pl.multiple_of(place * rows, rows), rows), :]
        for d in range(1, size):
            total = total + into[d - 1]
        return total

    acc[pl.ds(pl.multiple_of((1 - core) * 512, 512), 512), :] += product((1 - core) * 512, 512, 3)
    for h in (1, 0):
        c_copy(h).start()
    acc[pl.ds(pl.multiple_of(core * 512, 512), 512), :] += product(core * 512, 512, 3)

    round_wait(2)
    c_copy(1).wait_recv()
    bz_out[...] = acc[pl.ds(pl.multiple_of(core * 512 + 256, 256), 256), :] + core_in[1]
    for d in z_order:
        bz_copy(d).start()
    c_copy(0).wait_recv()
    ax_out[...] = acc[pl.ds(pl.multiple_of(core * 512, 256), 256), :] + core_in[0]
    for d in x_order:
        ax_copy(d).start()
    az_out[...] = gathered(ax_out, ax_in, ax_copy, x, NX)
    for d in z_order:
        az_copy(d).start()
    bx_out[...] = gathered(bz_out, bz_in, bz_copy, z, NZ)
    for d in x_order:
        bx_copy(d).start()
    y_out[8:16, :] = gathered(bx_out, bx_in, bx_copy, x, NX)
    y_out[0:8, :] = gathered(az_out, az_in, az_copy, z, NZ)

    y_rows = [1 - yh, 1 - yh, yh]

    def y_copy(k):
        return pltpu.make_async_remote_copy(
            src_ref=y_out.at[pl.ds(pl.multiple_of(y_rows[k] * 8, 8), 8), :], dst_ref=y_in.at[k],
            send_sem=y_send.at[k], recv_sem=y_recv.at[k], device_id=y_peer[k], device_id_type=MESH)

    for k in range(3):
        y_copy(k).start()
    for k in range(3):
        y_copy(k).wait_recv()
    mine = pl.ds(pl.multiple_of(8 * sub, 8), 8)
    others = pl.ds(pl.multiple_of(8 * (1 - sub), 8), 8)
    patch_v[mine, :] = y_out[pl.ds(pl.multiple_of(yh * 8, 8), 8), :] + y_in[0]
    patch_v[others, :] = y_in[1] + y_in[2]

    for copy in n_copy0:
        copy.wait_send()
    wait_a_send(psi0, 0)
    wait_a_send(psi1, 2)
    for d in range(8):
        n_copy1(d).wait_send()

    @pl.when(is_wall)
    def _():
        for k in range(4):
            s_copy(k).wait_send()

    for h in range(2):
        c_copy(h).wait_send()
    for d in range(1, NX):
        ax_copy(d).wait_send()
        bx_copy(d).wait_send()
    for d in range(1, NZ):
        az_copy(d).wait_send()
        bz_copy(d).wait_send()
    for k in range(3):
        y_copy(k).wait_send()
    state_copy.wait()


def hand_on(state_in, patch_in, state_out, patch_out, state, patch, in_sem, out_sem):
    pieces = [(patch_in, patch, patch_out)] + [(state_in.at[v], state.at[v], state_out.at[v]) for v in range(NV)]
    enter = [pltpu.make_async_copy(a, b, in_sem.at[n]) for n, (a, b, _) in enumerate(pieces)]
    leave = [pltpu.make_async_copy(b, c, out_sem.at[n]) for n, (_, b, c) in enumerate(pieces)]
    for copy in enter:
        copy.start()
    for n, copy in enumerate(enter):
        copy.wait()
        leave[n].start()
    for copy in leave:
        copy.wait()


def local(
    adjoint_start, objective_grad, flux_jacobian, stab_block, precond_block,
    wall_weight, wall_geometry, face_patch, patch_slot,
):
    any_, vmem = (pl.BlockSpec(memory_space=m) for m in (pl.ANY, pltpu.VMEM))
    dma = pltpu.SemaphoreType.DMA
    state, patch = pl.pallas_call(
        kernel,
        out_shape=(jax.ShapeDtypeStruct((NV, 256, 128), F32), jax.ShapeDtypeStruct((16, 128), F32)),
        in_specs=[any_] * 9,
        out_specs=(any_, vmem),
        scratch_shapes=[
            pltpu.VMEM((NV, 272, 128), F32),
            pltpu.VMEM((NV, 272, 128), F32),
            pltpu.VMEM((NV, 256, 128), F32),
            pltpu.VMEM((NV, 256, 128), F32),
            pltpu.VMEM((75, 256, 128), BF16),
            pltpu.VMEM((25, 256, 128), BF16),
            pltpu.VMEM((25, 256, 128), BF16),
            pltpu.VMEM((8192, 128), BF16),
            pltpu.SMEM((2, NV), F32),
            pltpu.VMEM((32, 128), jnp.int32),
            pltpu.VMEM((16, 128), jnp.int32),
            pltpu.VMEM((32, 256, 128), F32),
            pltpu.VMEM((1024, 4096), BF16),
            pltpu.VMEM((32, 128), jnp.int32),
            pltpu.VMEM((1024, 256), BF16),
            pltpu.VMEM((1024, 256), BF16),
            pltpu.VMEM((1024, 128), F32),
            pltpu.VMEM((NV, 32, 1, 128), F32),
            pltpu.VMEM((NV, 32, 1, 128), F32),
            pltpu.VMEM((NV, 32, 1, 128), F32),
            pltpu.VMEM((NV, 32, 1, 128), F32),
            pltpu.VMEM((2, 32, 128), F32),
            pltpu.VMEM((2, 32, 128), F32),
            pltpu.VMEM((2, 256, 128), F32),
            pltpu.VMEM((256, 128), F32),
            pltpu.VMEM((NX - 1, 64, 128), F32),
            pltpu.VMEM((64, 128), F32),
            pltpu.VMEM((NZ - 1, 8, 128), F32),
            pltpu.VMEM((256, 128), F32),
            pltpu.VMEM((NZ - 1, 32, 128), F32),
            pltpu.VMEM((32, 128), F32),
            pltpu.VMEM((NX - 1, 8, 128), F32),
            pltpu.VMEM((16, 128), F32),
            pltpu.VMEM((3, 8, 128), F32),
            pltpu.SemaphoreType.REGULAR((3,)),
            dma((5,)), dma((4 * len(PARTS),)), dma,
            dma((4,)), dma((4,)),
            dma((4,)), dma((4,)), dma((8,)), dma((8,)),
            dma((4,)), dma((4,)),
            dma((2,)), dma((2,)),
            dma((NX - 1,)), dma((NX - 1,)), dma((NZ - 1,)), dma((NZ - 1,)),
            dma((NZ - 1,)), dma((NZ - 1,)), dma((NX - 1,)), dma((NX - 1,)),
            dma((3,)), dma((3,)),
        ],
        compiler_params=pltpu.CompilerParams(
            collective_id=0, has_side_effects=True, vmem_limit_bytes=60 * 1024 * 1024),
    )(
        adjoint_start.reshape(NV, 256, 128),
        objective_grad.reshape(NV, 256, 128),
        flux_jacobian.reshape(75, 256, 128),
        stab_block.reshape(25, 256, 128),
        precond_block.reshape(25, 256, 128),
        wall_weight.T,
        wall_geometry.reshape(8192, 128),
        face_patch.reshape(32, 128),
        patch_slot.reshape(16, 128),
    )
    state, patch = pl.pallas_call(
        hand_on,
        out_shape=(jax.ShapeDtypeStruct(state.shape, F32), jax.ShapeDtypeStruct(patch.shape, F32)),
        in_specs=[any_, any_],
        out_specs=(any_, any_),
        scratch_shapes=[pltpu.VMEM((NV, 256, 128), F32), pltpu.VMEM((16, 128), F32), dma((6,)), dma((6,))],
        compiler_params=pltpu.CompilerParams(vmem_limit_bytes=60 * 1024 * 1024),
    )(state, patch)
    return state.reshape(NV, 32, 8, 128), patch


def solution(mesh):
    return jax.shard_map(
        local,
        mesh=mesh,
        in_specs=(
            P(None, "blk", "sub", None),
            P(None, "blk", "sub", None),
            P(None, None, None, "blk", "sub", None),
            P(None, None, "blk", "sub", None),
            P(None, None, "blk", "sub", None),
            P(),
            P("blk", None, None),
            P("blk"),
            P(),
        ),
        out_specs=(P(None, "blk", "sub", None), P("blk", None)),
        check_vma=False,
    )
```
